512 devices in a mesh: dp: 32 (over z, x), seq: 16 (over y, core).
Axes of the slice: x: 4, y: 8, z: 8, core: 2. Of those that a mesh axis runs over, the one named last changes fastest.
Arguments:
- patches: bfloat16 [32, 2048, 1792], P('dp', 'seq'), may hold values from -200 to 200
- cotangent: bfloat16 [32, 2048, 1792], P('dp', 'seq'), may hold values from -200 to 200
- pattern: int32 [24, 2], replicated, may hold values from 0 to 7, as said below
- weight: float32 [1792, 16, 336], P('dp', 'seq'), may hold values from -8 to 8
- first_moment: float32 [1792, 16, 336], P('dp', 'seq'), may hold values from -6 to 6
- second_moment: float32 [1792, 16, 336], P('dp', 'seq'), may hold values from 0.5 to 2
- layer_index: int32 [], replicated, may hold values from 40 to 55
Outputs:
- attn_out: bfloat16 [32, 2048, 1792], P('dp', 'seq')
- update: float32 [1792, 16, 336], P('dp', 'seq')
- new_first: float32 [1792, 16, 336], P('dp', 'seq')
- new_second: float32 [1792, 16, 336], P('dp', 'seq')
The draws below stay inside these ranges and needn't reach their ends.
Inputs may be any that keep to these rules, and one draw needn't show every extreme that they name: `pattern`: rows 3b, 3b + 1 and 3b + 2 hold query block b in their first entry; their second entries are three different key blocks: b itself, then b - 1 or b + 1, then one more block.
All inputs are finite; a program needn't handle non-finite values.
Results may differ from the reference program's by a relative error of at most 0.009.
Values may be sent and summed in bfloat16 or wider, within the bound.
No kernel may reach another device: no remote copies, remote signals or barrier semaphores. Data moves between devices by JAX's collectives and lax.ppermute only.
A program may use at most 64 MiB of HBM per device.

```python
import math
import jax
import jax.numpy as jnp
from jax import lax

D = 1792
HEADS = 16
HEAD_DIM = 112
DEPTH = 56
PATCHES = 2048
BLOCK = 256
STEP = 1000
IMAGES = 32


def feature_scales(scale_key, features):
    rough = jnp.exp(jax.random.uniform(scale_key, (features,), jnp.float32, 0.0, math.log(10.0)))
    trend = jnp.exp(math.log(3.0) * jnp.arange(features, dtype=jnp.float32) / features)
    return rough * trend


def image_profiles(tilt_key, images, features):
    tilts = jax.random.uniform(tilt_key, (images, 1, 1), jnp.float32, -3.0, 3.0)
    place = jnp.arange(features, dtype=jnp.float32) / features - 0.5
    return jnp.exp(tilts * place[None, None, :])


def draw_patches(key, part):
    key = jax.random.fold_in(key, 11)
    scale_key = jax.random.fold_in(key, 0)
    main_key = jax.random.fold_in(key, 1)
    tilt_key = jax.random.fold_in(key, 4)
    scales = feature_scales(scale_key, D)
    profiles = image_profiles(tilt_key, IMAGES, D)
    tokens = jnp.clip(jax.random.normal(main_key, (IMAGES, PATCHES, D), jnp.float32), -6.0, 6.0)
    return jnp.clip(tokens * scales * profiles, -200.0, 200.0).astype(jnp.bfloat16)


def draw_cotangent(key, part):
    key = jax.random.fold_in(key, 13)
    scale_key = jax.random.fold_in(key, 0)
    main_key = jax.random.fold_in(key, 1)
    tilt_key = jax.random.fold_in(key, 3)
    scales = feature_scales(scale_key, D)
    profiles = image_profiles(tilt_key, IMAGES, D)
    tokens = jnp.clip(jax.random.normal(main_key, (IMAGES, PATCHES, D), jnp.float32), -6.0, 6.0)
    return jnp.clip(tokens * scales * profiles, -200.0, 200.0).astype(jnp.bfloat16)


def draw_pattern(key, part):
    key = jax.random.fold_in(key, 23)
    side_key, far_key = jax.random.split(key)
    blocks = PATCHES // BLOCK
    own = jnp.arange(blocks, dtype=jnp.int32)
    coin = jax.random.randint(side_key, (blocks,), 0, 2, dtype=jnp.int32)
    offset = jnp.where(own == 0, 1, jnp.where(own == blocks - 1, -1, 2 * coin - 1))
    near = own + offset
    lower = jnp.minimum(own, near)
    upper = jnp.maximum(own, near)
    picked = jax.random.randint(far_key, (blocks,), 0, blocks - 2, dtype=jnp.int32)
    remote = picked + (picked >= lower).astype(jnp.int32)
    remote = remote + (remote >= upper).astype(jnp.int32)
    key_blocks = jnp.stack([own, near, remote], axis=1).reshape(-1)
    query_blocks = jnp.repeat(own, 3)
    return jnp.stack([query_blocks, key_blocks], axis=1).astype(jnp.int32)


def draw_weight(key, part):
    key = jax.random.fold_in(key, 17)
    main_key = jax.random.fold_in(key, 0)
    head_key = jax.random.fold_in(key, 3)
    base = jnp.clip(jax.random.normal(main_key, (D, HEADS, 3 * HEAD_DIM), jnp.float32), -6.0, 6.0)
    head_scale = jnp.exp(jax.random.uniform(head_key, (1, HEADS, 1), jnp.float32, 0.0, math.log(8.0)))
    factors = jnp.concatenate([jnp.ones((1, HEADS, 2 * HEAD_DIM), jnp.float32), jnp.broadcast_to(head_scale, (1, HEADS, HEAD_DIM))], axis=2)
    return base * factors * D ** (-0.5)


def shard_levels(key, shape, cuts, low, high):
    loudness, own = 1.0, jax.random.fold_in(key, 6)
    for axis_at, parts in cuts:
        steps = jnp.exp(jax.random.uniform(jax.random.fold_in(own, axis_at), (parts,), jnp.float32, low / len(cuts), high / len(cuts)))
        loudness = loudness * jnp.repeat(steps, shape[axis_at] // parts).reshape([-1 if axis == axis_at else 1 for axis in range(len(shape))])
    return loudness


def noise(stream_key, shape, width, reach, shards=(), kind=jnp.bfloat16):
    drawn = width * jax.random.normal(stream_key, shape, jnp.float32)
    if shards:
        drawn = drawn * shard_levels(stream_key, shape, shards, -0.22, 0.18)
    return jnp.clip(drawn, -reach, reach).astype(kind)


def setup_inputs(seed: int = 0) -> dict:
    splits = jax.random.split(jax.random.key(seed), 8)
    return {
        "patches": draw_patches(jax.random.fold_in(splits[7], 71), 0),
        "cotangent": draw_cotangent(jax.random.fold_in(splits[7], 71), 0),
        "pattern": draw_pattern(jax.random.fold_in(splits[7], 71), 0),
        "weight": draw_weight(jax.random.fold_in(splits[7], 71), 0),
        "first_moment": noise(splits[4], (D, HEADS, 3 * HEAD_DIM), 1.0, 6.0, ((0, 32), (1, 16)), jnp.float32),
        "second_moment": jnp.clip(jnp.exp(math.log(2.0) - 1.3862944 * jax.random.uniform(splits[5], (D, HEADS, 3 * HEAD_DIM), jnp.float32) ** shard_levels(splits[5], (D, HEADS, 3 * HEAD_DIM), ((0, 32), (1, 16)), -0.2, 0.2)), 0.5, 2.0),
        "layer_index": jax.random.randint(splits[6], (), 40, 56).astype(jnp.int32),
    }


norm_epsilon = 1e-06
clip_epsilon = 1e-06
first_decay = 0.9
second_decay = 0.999
adam_epsilon = 1e-08
weight_decay = 0.05
layer_decay = 0.9

def layer_norm(tokens):
    floats = tokens.astype(jnp.float32)
    centred = floats - lax.optimization_barrier(jnp.mean(floats, axis=-1, keepdims=True))
    spread = lax.optimization_barrier(jnp.mean(centred * centred, axis=-1, keepdims=True))
    return (centred * lax.rsqrt(spread + norm_epsilon)).astype(jnp.bfloat16)

def head_attend(projected, out_grads, pattern):
    length, triple = projected.shape
    head_dim = triple // 3
    blocks = pattern.shape[0] // 3
    block_len = length // blocks
    score_scale = head_dim ** (-0.5)
    queries = projected[:, :head_dim].reshape(blocks // 2, 2, block_len, head_dim)
    key_rows = projected[:, head_dim:2 * head_dim].reshape(blocks, block_len, head_dim)
    value_rows = projected[:, 2 * head_dim:].reshape(blocks, block_len, head_dim)
    chosen = pattern[:, 1].reshape(blocks, 3)
    near_keys = key_rows[chosen].reshape(blocks // 2, 2, 3 * block_len, head_dim)
    near_values = value_rows[chosen].reshape(blocks // 2, 2, 3 * block_len, head_dim)
    grads_in = out_grads.reshape(blocks // 2, 2, block_len, head_dim)

    def attend_group(member):
        group_q, group_k, group_v, group_g = [operand.astype(jnp.float32) for operand in member]
        scores = jnp.einsum('gqe,gke->gqk', group_q, group_k) * score_scale
        row_max = lax.optimization_barrier(jnp.max(scores, axis=-1, keepdims=True))
        shifted = jnp.exp(scores - row_max)
        soft_weights = shifted / lax.optimization_barrier(jnp.sum(shifted, axis=-1, keepdims=True))
        soft_low = lax.optimization_barrier(soft_weights.astype(jnp.bfloat16)).astype(jnp.float32)
        attended = jnp.einsum('gqk,gke->gqe', soft_low, group_v).astype(jnp.bfloat16)
        value_terms = jnp.einsum('gqk,gqe->gke', soft_low, group_g)
        prob_grads = jnp.einsum('gqe,gke->gqk', group_g, group_v)
        row_dot = lax.optimization_barrier(jnp.sum(soft_weights * prob_grads, axis=-1, keepdims=True))
        score_low = (soft_weights * (prob_grads - row_dot) * score_scale).astype(jnp.bfloat16)
        score_grads = lax.optimization_barrier(score_low).astype(jnp.float32)
        query_grads = jnp.einsum('gqk,gke->gqe', score_grads, group_k).astype(jnp.bfloat16)
        key_terms = jnp.einsum('gqk,gqe->gke', score_grads, group_q)
        return (attended, query_grads, key_terms, value_terms)
    attended, query_grads, key_terms, value_terms = lax.map(attend_group, (queries, near_keys, near_values, grads_in))
    onehot = (pattern[:, 1][None, :] == jnp.arange(blocks, dtype=jnp.int32)[:, None]).astype(jnp.float32)
    key_terms = key_terms.reshape(3 * blocks, block_len, head_dim)
    value_terms = value_terms.reshape(3 * blocks, block_len, head_dim)
    key_grads = jnp.einsum('np,pse->nse', onehot, key_terms, precision=lax.Precision.HIGHEST)
    value_grads = jnp.einsum('np,pse->nse', onehot, value_terms, precision=lax.Precision.HIGHEST)
    joined = jnp.concatenate([query_grads.reshape(length, head_dim), key_grads.astype(jnp.bfloat16).reshape(length, head_dim), value_grads.astype(jnp.bfloat16).reshape(length, head_dim)], axis=1)
    return (attended.reshape(length, head_dim), joined)

def reference(patches, cotangent, pattern, weight, first_moment, second_moment, layer_index):
    triple = 3 * HEAD_DIM
    weight_low = weight.astype(jnp.bfloat16).reshape(D, HEADS * triple)

    def per_image(carry, member):
        image_tokens, image_grads = member
        normed = layer_norm(image_tokens)
        projected = jnp.dot(normed, weight_low, preferred_element_type=jnp.float32).astype(jnp.bfloat16)
        projected = projected.reshape(PATCHES, HEADS, triple).transpose(1, 0, 2)
        head_grads = image_grads.reshape(PATCHES, HEADS, HEAD_DIM).transpose(1, 0, 2)
        attended, joined = lax.map(lambda member_h: head_attend(member_h[0], member_h[1], pattern), (projected, head_grads))
        attended = attended.transpose(1, 0, 2).reshape(PATCHES, D)
        joined = joined.transpose(1, 0, 2).reshape(PATCHES, HEADS * triple)
        carry = carry + jnp.dot(normed.T, joined, preferred_element_type=jnp.float32)
        return (carry, attended)
    start = jnp.zeros((D, HEADS * triple), jnp.float32)
    grad_weight, attn_out = lax.scan(per_image, start, (patches, cotangent))
    grad_weight = grad_weight.reshape(D, HEADS, triple)
    entries = D * HEADS * triple
    clip_factor = lax.rsqrt(jnp.sum(grad_weight * grad_weight) / entries + clip_epsilon)
    clipped = grad_weight * clip_factor
    new_first = first_decay * first_moment + (1.0 - first_decay) * clipped
    new_second = second_decay * second_moment + (1.0 - second_decay) * clipped * clipped
    rate = jnp.power(jnp.float32(layer_decay), (DEPTH - 1 - layer_index).astype(jnp.float32))
    first_hat = new_first / (1.0 - first_decay ** STEP)
    second_hat = new_second / (1.0 - second_decay ** STEP)
    update = rate * (first_hat / (jnp.sqrt(second_hat) + adam_epsilon) + weight_decay * weight)
    return (attn_out, update, new_first, new_second)
```

```python
import jax
import jax.numpy as jnp
from jax import lax
from jax.experimental import pallas as pl
from jax.experimental.pallas import tpu as pltpu
from jax.sharding import PartitionSpec as P

D = 1792
HEADS = 16
HEAD_DIM = 112
DEPTH = 56
STEP = 1000
PATCHES = 2048
BLOCK = 256
BLOCKS = PATCHES // BLOCK
LANES = 128
SLOTS = 3 * LANES
DP = 32
SEQ = 16
ROWS = PATCHES // SEQ
FEATS = D // DP

norm_epsilon = 1e-06
clip_epsilon = 1e-06
first_decay = 0.9
second_decay = 0.999
adam_epsilon = 1e-08
weight_decay = 0.05
layer_decay = 0.9
score_scale = HEAD_DIM ** (-0.5)

f32 = jnp.float32
bf16 = jnp.bfloat16
VMEM = pl.BlockSpec(memory_space=pltpu.VMEM)
SMEM = pl.BlockSpec(memory_space=pltpu.SMEM)
ANY = pl.BlockSpec(memory_space=pl.ANY)


def params(megabytes):
    return pltpu.CompilerParams(vmem_limit_bytes=megabytes * 2**20)


def norm_kernel(patch_ref, normed_ref):
    for start in range(0, ROWS, 32):
        rows = pl.ds(start, 32)
        floats = patch_ref[rows, :].astype(f32)
        centred = floats - jnp.mean(floats, axis=-1, keepdims=True)
        spread = jnp.mean(centred * centred, axis=-1, keepdims=True)
        normed_ref[rows, :] = (centred * lax.rsqrt(spread + norm_epsilon)).astype(bf16)


def split_kernel(grad_ref, slabs_ref):
    empty = jnp.zeros((ROWS, LANES - HEAD_DIM), bf16)
    for head in range(HEADS):
        part = grad_ref[:, head * HEAD_DIM : (head + 1) * HEAD_DIM]
        slabs_ref[head] = jnp.concatenate([part, empty], axis=1)


def join_kernel(slabs_ref, out_ref):
    out_ref[...] = jnp.concatenate([slabs_ref[head][:, :HEAD_DIM] for head in range(HEADS)], axis=1)


def dot(left, right):
    return lax.dot_general(left, right, (((1,), (0,)), ((), ())), preferred_element_type=f32)


def head_kernel(
    chosen_ref, tokens_hbm, weight_ref, grads_ref, attended_ref, grad_ref,
    tokens, keys, values, queries_t, keys_t, values_t, grads_t,
    key_grads, value_grads, joined_t, grad_rows, sems,
):
    copies = [
        pltpu.make_async_copy(
            tokens_hbm.at[pl.ds(b * BLOCK, BLOCK)], tokens.at[pl.ds(b * BLOCK, BLOCK)], sems.at[b]
        )
        for b in range(BLOCKS)
    ]
    for copy in copies:
        copy.start()
    key_grads[...] = jnp.zeros_like(key_grads)
    value_grads[...] = jnp.zeros_like(value_grads)
    for b in range(BLOCKS):
        rows = pl.ds(b * BLOCK, BLOCK)
        grads_t[:, rows] = grads_ref[rows, :].T
        copies[b].wait()
        projected = dot(tokens[rows, :], weight_ref[...]).astype(bf16)
        key = projected[:, LANES : 2 * LANES]
        value = projected[:, 2 * LANES :]
        keys[rows, :] = key
        values[rows, :] = value
        queries_t[:, rows] = projected[:, :LANES].T
        keys_t[:, rows] = key.T
        values_t[:, rows] = value.T

    def attend(b, carry):
        here = pl.ds(pl.multiple_of(b * BLOCK, BLOCK), BLOCK)
        query_t = queries_t[:, here]
        grad_t = grads_t[:, here]
        places = [pl.ds(pl.multiple_of(chosen_ref[3 * b + j] * BLOCK, BLOCK), BLOCK) for j in range(3)]
        scores = [dot(keys[place, :], query_t) * score_scale for place in places]
        top = jnp.max(jnp.maximum(jnp.maximum(scores[0], scores[1]), scores[2]), axis=0, keepdims=True)
        shifted = [jnp.exp(score - top) for score in scores]
        total = jnp.sum(shifted[0] + shifted[1] + shifted[2], axis=0, keepdims=True)
        soft = [part / total for part in shifted]
        soft_low = [part.astype(bf16) for part in soft]
        attended_t = sum(dot(values_t[:, place], low) for place, low in zip(places, soft_low))
        attended_ref[here, :] = attended_t.T.astype(bf16)
        prob_grads = [dot(values[place, :], grad_t) for place in places]
        row_dot = jnp.sum(
            soft[0] * prob_grads[0] + soft[1] * prob_grads[1] + soft[2] * prob_grads[2], axis=0, keepdims=True
        )
        score_grads = [
            (part * (prob - row_dot) * score_scale).astype(bf16) for part, prob in zip(soft, prob_grads)
        ]
        query_grads_t = sum(dot(keys_t[:, place], part) for place, part in zip(places, score_grads))
        joined_t[:LANES, here] = query_grads_t.astype(bf16)
        query = query_t.T
        grad = grads_ref[here, :]
        for place, low, part in zip(places, soft_low, score_grads):
            value_grads[place, :] += dot(low, grad)
            key_grads[place, :] += dot(part, query)
        return carry

    lax.fori_loop(0, BLOCKS, attend, 0)
    for b in range(BLOCKS):
        rows = pl.ds(b * BLOCK, BLOCK)
        joined_t[LANES : 2 * LANES, rows] = key_grads[rows, :].astype(bf16).T
        joined_t[2 * LANES :, rows] = value_grads[rows, :].astype(bf16).T
    for start in range(0, D, 2 * LANES):
        part = dot(joined_t[...], tokens[:, start : start + 2 * LANES])
        grad_rows[start : start + 2 * LANES, :] = part.T
    for chunk in range(DP):
        grad_ref[chunk] = grad_rows[chunk * FEATS : (chunk + 1) * FEATS, :].astype(bf16)


def head_call(chosen, tokens, weight_low, grads):
    return pl.pallas_call(
        head_kernel,
        out_shape=(
            jax.ShapeDtypeStruct((PATCHES, LANES), bf16),
            jax.ShapeDtypeStruct((DP, FEATS, SLOTS), bf16),
        ),
        in_specs=[SMEM, ANY, VMEM, VMEM],
        out_specs=(VMEM, VMEM),
        scratch_shapes=[
            pltpu.VMEM((PATCHES, D), bf16),
            pltpu.VMEM((PATCHES, LANES), bf16),
            pltpu.VMEM((PATCHES, LANES), bf16),
            pltpu.VMEM((LANES, PATCHES), bf16),
            pltpu.VMEM((LANES, PATCHES), bf16),
            pltpu.VMEM((LANES, PATCHES), bf16),
            pltpu.VMEM((LANES, PATCHES), bf16),
            pltpu.VMEM((PATCHES, LANES), f32),
            pltpu.VMEM((PATCHES, LANES), f32),
            pltpu.VMEM((SLOTS, PATCHES), bf16),
            pltpu.VMEM((D, SLOTS), f32),
            pltpu.SemaphoreType.DMA((BLOCKS,)),
        ],
        compiler_params=params(60),
        name="head",
    )(chosen, tokens, weight_low, grads)


def small_call(kernel, out_shape, *arrays):
    return pl.pallas_call(
        kernel,
        out_shape=out_shape,
        in_specs=[VMEM] * len(arrays),
        out_specs=VMEM,
        compiler_params=params(16),
    )(*arrays)


def local(patches, cotangent, pattern, weight, first_moment, second_moment, layer_index):
    normed = small_call(norm_kernel, jax.ShapeDtypeStruct((ROWS, D), bf16), patches[0])
    gathered = lax.all_gather(normed, "seq", axis=0, tiled=True)

    weight_low = jnp.pad(
        weight.astype(bf16).reshape(FEATS, 3, HEAD_DIM), ((0, 0), (0, 0), (0, LANES - HEAD_DIM))
    ).reshape(1, FEATS, SLOTS)
    weight_all = lax.all_to_all(
        jnp.broadcast_to(weight_low, (DP, FEATS, SLOTS)), "dp", 0, 0, tiled=True
    ).reshape(D, SLOTS)
    slabs = small_call(split_kernel, jax.ShapeDtypeStruct((HEADS, ROWS, LANES), bf16), cotangent[0])
    grads = lax.all_to_all(slabs, "seq", 0, 0, tiled=True).reshape(PATCHES, LANES)

    attended, grad_parts = head_call(pattern[:, 1], gathered, weight_all, grads)

    received = lax.all_to_all(grad_parts, "dp", 0, 0, tiled=True)
    grad = jnp.sum(received.astype(f32), axis=0)
    squares = jnp.broadcast_to(jnp.sum(grad * grad), (DP, LANES))
    squares = jnp.sum(lax.all_to_all(squares, "dp", 0, 0, tiled=True), axis=0)
    squares = lax.all_to_all(jnp.broadcast_to(squares, (SEQ, LANES)), "seq", 0, 0, tiled=True)
    squares = jnp.sum(squares, axis=0)[0]

    returned = lax.all_to_all(attended.reshape(SEQ, ROWS, LANES), "seq", 0, 0, tiled=True)
    attn_out = small_call(join_kernel, jax.ShapeDtypeStruct((ROWS, D), bf16), returned)

    grad = grad.reshape(FEATS, 3, LANES)[:, :, :HEAD_DIM].reshape(weight.shape)
    clip_factor = lax.rsqrt(squares / (D * HEADS * 3 * HEAD_DIM) + clip_epsilon)
    clipped = grad * clip_factor
    new_first = first_decay * first_moment + (1.0 - first_decay) * clipped
    new_second = second_decay * second_moment + (1.0 - second_decay) * clipped * clipped
    rate = jnp.power(f32(layer_decay), (DEPTH - 1 - layer_index).astype(f32))
    first_hat = new_first / (1.0 - first_decay**STEP)
    second_hat = new_second / (1.0 - second_decay**STEP)
    update = rate * (first_hat / (jnp.sqrt(second_hat) + adam_epsilon) + weight_decay * weight)
    return (attn_out[None], update, new_first, new_second)


def solution(mesh):
    split = P("dp", "seq", None)
    return jax.shard_map(
        local,
        mesh=mesh,
        in_specs=(split, split, P(), split, split, split, P()),
        out_specs=(split, split, split, split),
        check_vma=False,
    )
```

```python
import jax
import jax.numpy as jnp
from jax import lax
from jax.experimental import pallas as pl
from jax.experimental.pallas import tpu as pltpu
from jax.sharding import Mesh
from jax.sharding import PartitionSpec as P

D = 1792
HEADS = 16
HEAD_DIM = 112
DEPTH = 56
STEP = 1000
PATCHES = 2048
BLOCK = 256
BLOCKS = PATCHES // BLOCK
LANES = 128
SLOTS = 3 * LANES
DP = 32
SEQ = 16
ROWS = PATCHES // SEQ
FEATS = D // DP
Z, X, Y, CORES = 4, 8, 8, 2
SPLIT = X * FEATS

norm_epsilon = 1e-06
clip_epsilon = 1e-06
first_decay = 0.9
second_decay = 0.999
adam_epsilon = 1e-08
weight_decay = 0.05
layer_decay = 0.9
score_scale = HEAD_DIM ** (-0.5)

f32 = jnp.float32
bf16 = jnp.bfloat16
VMEM = pl.BlockSpec(memory_space=pltpu.VMEM)
SMEM = pl.BlockSpec(memory_space=pltpu.SMEM)
ANY = pl.BlockSpec(memory_space=pl.ANY)


def params(megabytes):
    return pltpu.CompilerParams(vmem_limit_bytes=megabytes * 2**20)


def norm_kernel(patch_ref, normed_ref):
    for start in range(0, ROWS, 32):
        rows = pl.ds(start, 32)
        floats = patch_ref[rows, :].astype(f32)
        centred = floats - jnp.mean(floats, axis=-1, keepdims=True)
        spread = jnp.mean(centred * centred, axis=-1, keepdims=True)
        normed_ref[rows, :] = (centred * lax.rsqrt(spread + norm_epsilon)).astype(bf16)


def split_kernel(grad_ref, slabs_ref):
    empty = jnp.zeros((ROWS, LANES - HEAD_DIM), bf16)
    for head in range(HEADS):
        part = grad_ref[:, head * HEAD_DIM : (head + 1) * HEAD_DIM]
        slabs_ref[head] = jnp.concatenate([part, empty], axis=1)


def join_kernel(place_ref, *refs):
    part_refs, out_ref, slabs = refs[:Y], refs[Y], refs[Y + 1]
    y, core = place_ref[1], place_ref[2]
    for k, part_ref in enumerate(part_refs):
        first = 2 * lax.rem(y + Y - k, Y)
        slabs[first + core] = part_ref[0]
        slabs[first + 1 - core] = part_ref[1]
    out_ref[...] = jnp.concatenate([slabs[head][:, :HEAD_DIM] for head in range(HEADS)], axis=1)


def dot(left, right):
    return lax.dot_general(left, right, (((1,), (0,)), ((), ())), preferred_element_type=f32)


def head_kernel(
    chosen_ref, place_ref, tokens_hbm, weight_0, weight_1, weight_3, weight_2a, weight_2b, grads_ref,
    attended_ref, grad_ref,
    tokens, weights, keys, values, queries_t, keys_t, values_t, grads_t,
    key_grads, value_grads, joined_t, grad_rows, sems,
):
    copies = [
        pltpu.make_async_copy(
            tokens_hbm.at[pl.ds(b * BLOCK, BLOCK)], tokens.at[pl.ds(b * BLOCK, BLOCK)], sems.at[b]
        )
        for b in range(BLOCKS)
    ]
    for copy in copies:
        copy.start()
    z, y, core = place_ref[0], place_ref[1], place_ref[2]

    def weight_rows(k, start, size):
        return pl.ds(pl.multiple_of(lax.rem(z + k, Z) * SPLIT, 64) + start, size)

    weights[weight_rows(0, 0, SPLIT), :] = weight_0[...]
    weights[weight_rows(1, 0, SPLIT), :] = weight_1[...]
    weights[weight_rows(3, 0, SPLIT), :] = weight_3[...]
    weights[weight_rows(2, 0, SPLIT // 2), :] = weight_2a[...]
    weights[weight_rows(2, SPLIT // 2, SPLIT // 2), :] = weight_2b[...]
    key_grads[...] = jnp.zeros_like(key_grads)
    value_grads[...] = jnp.zeros_like(value_grads)
    for b in range(BLOCKS):
        rows = pl.ds(b * BLOCK, BLOCK)
        grads_t[:, rows] = grads_ref[rows, :].T
        copies[b].wait()
        projected = dot(tokens[rows, :], weights[...]).astype(bf16)
        key = projected[:, LANES : 2 * LANES]
        value = projected[:, 2 * LANES :]
        keys[rows, :] = key
        values[rows, :] = value
        queries_t[:, rows] = projected[:, :LANES].T
        keys_t[:, rows] = key.T
        values_t[:, rows] = value.T

    def attend(b, carry):
        here = pl.ds(pl.multiple_of(b * BLOCK, BLOCK), BLOCK)
        query_t = queries_t[:, here]
        grad_t = grads_t[:, here]
        places = [pl.ds(pl.multiple_of(chosen_ref[3 * b + j] * BLOCK, BLOCK), BLOCK) for j in range(3)]
        scores = [dot(keys[place, :], query_t) * score_scale for place in places]
        top = jnp.max(jnp.maximum(jnp.maximum(scores[0], scores[1]), scores[2]), axis=0, keepdims=True)
        shifted = [jnp.exp(score - top) for score in scores]
        total = jnp.sum(shifted[0] + shifted[1] + shifted[2], axis=0, keepdims=True)
        soft = [part / total for part in shifted]
        soft_low = [part.astype(bf16) for part in soft]
        attended_t = sum(dot(values_t[:, place], low) for place, low in zip(places, soft_low))
        attended = attended_t.T.astype(bf16)
        ahead = lax.rem(b + Y - y, Y)
        attended_ref[core, ahead] = attended[:ROWS]
        attended_ref[1 - core, ahead] = attended[ROWS:]
        prob_grads = [dot(values[place, :], grad_t) for place in places]
        row_dot = jnp.sum(
            soft[0] * prob_grads[0] + soft[1] * prob_grads[1] + soft[2] * prob_grads[2], axis=0, keepdims=True
        )
        score_grads = [
            (part * (prob - row_dot) * score_scale).astype(bf16) for part, prob in zip(soft, prob_grads)
        ]
        query_grads_t = sum(dot(keys_t[:, place], part) for place, part in zip(places, score_grads))
        joined_t[:LANES, here] = query_grads_t.astype(bf16)
        query = query_t.T
        grad = grads_ref[here, :]
        for place, low, part in zip(places, soft_low, score_grads):
            value_grads[place, :] += dot(low, grad)
            key_grads[place, :] += dot(part, query)
        return carry

    lax.fori_loop(0, BLOCKS, attend, 0)
    for b in range(BLOCKS):
        rows = pl.ds(b * BLOCK, BLOCK)
        joined_t[LANES : 2 * LANES, rows] = key_grads[rows, :].astype(bf16).T
        joined_t[2 * LANES :, rows] = value_grads[rows, :].astype(bf16).T
    for start in range(0, D, 2 * LANES):
        part = dot(joined_t[...], tokens[:, start : start + 2 * LANES])
        grad_rows[start : start + 2 * LANES, :] = part.T
    for chunk in range(DP):
        grad_ref[chunk] = grad_rows[chunk * FEATS : (chunk + 1) * FEATS, :].astype(bf16)


def head_call(chosen, place, tokens, weight_parts, grads):
    return pl.pallas_call(
        head_kernel,
        out_shape=(
            jax.ShapeDtypeStruct((CORES, Y, ROWS, LANES), bf16),
            jax.ShapeDtypeStruct((DP, FEATS, SLOTS), bf16),
        ),
        in_specs=[SMEM, SMEM, ANY] + [VMEM] * 6,
        out_specs=(VMEM, VMEM),
        scratch_shapes=[
            pltpu.VMEM((PATCHES, D), bf16),
            pltpu.VMEM((D, SLOTS), bf16),
            pltpu.VMEM((PATCHES, LANES), bf16),
            pltpu.VMEM((PATCHES, LANES), bf16),
            pltpu.VMEM((LANES, PATCHES), bf16),
            pltpu.VMEM((LANES, PATCHES), bf16),
            pltpu.VMEM((LANES, PATCHES), bf16),
            pltpu.VMEM((LANES, PATCHES), bf16),
            pltpu.VMEM((PATCHES, LANES), f32),
            pltpu.VMEM((PATCHES, LANES), f32),
            pltpu.VMEM((SLOTS, PATCHES), bf16),
            pltpu.VMEM((D, SLOTS), f32),
            pltpu.SemaphoreType.DMA((BLOCKS,)),
        ],
        compiler_params=params(60),
        name="head",
    )(chosen, place, tokens, *weight_parts, grads)


def join_call(place, parts):
    return pl.pallas_call(
        join_kernel,
        out_shape=jax.ShapeDtypeStruct((ROWS, D), bf16),
        in_specs=[SMEM] + [VMEM] * Y,
        out_specs=VMEM,
        scratch_shapes=[pltpu.VMEM((HEADS, ROWS, LANES), bf16)],
        compiler_params=params(16),
        name="join",
    )(place, *parts)


def ring(size, step):
    return [(at, (at + step) % size) for at in range(size)]


def gather_weights(weight_low):
    near = lax.all_to_all(
        jnp.broadcast_to(weight_low, (X, FEATS, SLOTS)), "x", 0, 0, tiled=True
    ).reshape(SPLIT, SLOTS)
    following = lax.ppermute(near, "z", ring(Z, -1))
    previous = lax.ppermute(near, "z", ring(Z, 1))
    far_first = lax.ppermute(following[: SPLIT // 2], "z", ring(Z, -1))
    far_second = lax.ppermute(previous[SPLIT // 2 :], "z", ring(Z, 1))
    return (near, following, previous, far_first, far_second)


def return_heads(attended):
    swapped = lax.ppermute(attended[1], "c", ring(CORES, 1))
    pairs = [jnp.stack([attended[0, k], swapped[k]]) for k in range(Y)]
    return [pairs[0]] + [lax.ppermute(pairs[k], "y", ring(Y, k)) for k in range(1, Y)]


def small_call(kernel, out_shape, *arrays):
    return pl.pallas_call(
        kernel,
        out_shape=out_shape,
        in_specs=[VMEM] * len(arrays),
        out_specs=VMEM,
        compiler_params=params(16),
    )(*arrays)


def local(patches, cotangent, pattern, weight, first_moment, second_moment, layer_index):
    place = jnp.stack([lax.axis_index("z"), lax.axis_index("y"), lax.axis_index("c")]).astype(jnp.int32)
    normed = small_call(norm_kernel, jax.ShapeDtypeStruct((ROWS, D), bf16), patches[0])
    gathered = lax.all_gather(normed, ("y", "c"), axis=0, tiled=True)

    weight_low = jnp.pad(
        weight.astype(bf16).reshape(FEATS, 3, HEAD_DIM), ((0, 0), (0, 0), (0, LANES - HEAD_DIM))
    ).reshape(1, FEATS, SLOTS)
    weight_parts = gather_weights(weight_low)
    slabs = small_call(split_kernel, jax.ShapeDtypeStruct((HEADS, ROWS, LANES), bf16), cotangent[0])
    grads = lax.all_to_all(slabs, ("y", "c"), 0, 0, tiled=True).reshape(PATCHES, LANES)

    attended, grad_parts = head_call(pattern[:, 1], place, gathered, weight_parts, grads)

    received = lax.all_to_all(grad_parts, ("z", "x"), 0, 0, tiled=True)
    received, *returned = lax.optimization_barrier((received, *return_heads(attended)))
    attn_out = join_call(place, returned)
    grad = jnp.sum(received.astype(f32), axis=0)
    squares = jnp.broadcast_to(jnp.sum(grad * grad), (DP, LANES))
    squares = jnp.sum(lax.all_to_all(squares, ("z", "x"), 0, 0, tiled=True), axis=0)
    squares = lax.all_to_all(jnp.broadcast_to(squares, (SEQ, LANES)), ("y", "c"), 0, 0, tiled=True)
    squares = jnp.sum(squares, axis=0)[0]

    grad = grad.reshape(FEATS, 3, LANES)[:, :, :HEAD_DIM].reshape(weight.shape)
    clip_factor = lax.rsqrt(squares / (D * HEADS * 3 * HEAD_DIM) + clip_epsilon)
    clipped = grad * clip_factor
    new_first = first_decay * first_moment + (1.0 - first_decay) * clipped
    new_second = second_decay * second_moment + (1.0 - second_decay) * clipped * clipped
    rate = jnp.power(f32(layer_decay), (DEPTH - 1 - layer_index).astype(f32))
    first_hat = new_first / (1.0 - first_decay**STEP)
    second_hat = new_second / (1.0 - second_decay**STEP)
    update = rate * (first_hat / (jnp.sqrt(second_hat) + adam_epsilon) + weight_decay * weight)
    return (attn_out[None], update, new_first, new_second)


def solution(mesh):
    named = Mesh(mesh.devices.reshape(Z, X, Y, CORES), ("z", "x", "y", "c"))
    split = P(("z", "x"), ("y", "c"), None)
    return jax.shard_map(
        local,
        mesh=named,
        in_specs=(split, split, P(), split, split, split, P()),
        out_specs=(split, split, split, split),
        check_vma=False,
    )
```

```python
import jax
import jax.numpy as jnp
from jax import lax
from jax.experimental import pallas as pl
from jax.experimental.pallas import tpu as pltpu
from jax.sharding import Mesh
from jax.sharding import PartitionSpec as P

D = 1792
HEADS = 16
HEAD_DIM = 112
DEPTH = 56
STEP = 1000
PATCHES = 2048
BLOCK = 256
BLOCKS = PATCHES // BLOCK
LANES = 128
SLOTS = 3 * LANES
DP = 32
SEQ = 16
ROWS = PATCHES // SEQ
FEATS = D // DP
Z, X, Y, CORES = 4, 8, 8, 2

norm_epsilon = 1e-06
clip_epsilon = 1e-06
first_decay = 0.9
second_decay = 0.999
adam_epsilon = 1e-08
weight_decay = 0.05
layer_decay = 0.9
LOG2E = 1.4426950408889634
score_scale = HEAD_DIM ** (-0.5)

f32 = jnp.float32
bf16 = jnp.bfloat16
VMEM = pl.BlockSpec(memory_space=pltpu.VMEM)
SMEM = pl.BlockSpec(memory_space=pltpu.SMEM)
HBM = pl.BlockSpec(memory_space=pltpu.HBM)


def params(megabytes):
    return pltpu.CompilerParams(vmem_limit_bytes=megabytes * 2**20)


def norm_kernel(patch_ref, normed_ref):
    for start in range(0, ROWS, 32):
        rows = pl.ds(start, 32)
        floats = patch_ref[rows, :].astype(f32)
        centred = floats - jnp.mean(floats, axis=-1, keepdims=True)
        spread = jnp.mean(centred * centred, axis=-1, keepdims=True)
        normed_ref[rows, :] = (centred * lax.rsqrt(spread + norm_epsilon)).astype(bf16)


def split_kernel(grad_ref, slabs_ref):
    empty = jnp.zeros((ROWS, LANES - HEAD_DIM), bf16)
    for head in range(HEADS):
        part = grad_ref[:, head * HEAD_DIM : (head + 1) * HEAD_DIM]
        slabs_ref[head] = jnp.concatenate([part, empty], axis=1)


def place_kernel(place_ref, *refs):
    block_refs, weights_ref, rows_ref = refs[:-2], refs[-2], refs[-1]
    z, x = place_ref[2], place_ref[3]
    for block_ref, shift, first in zip(block_refs, (0, -1, -2, -3, 1, 2, 3, 4, 4), (0,) * 8 + (2,)):
        for k in range(block_ref.shape[0]):
            owner = lax.rem(z + first + k, Z) * X + lax.rem(x + shift + X, X)
            rows_ref[pl.ds(pl.multiple_of(owner * FEATS, 8), FEATS), :] = block_ref[k].astype(f32)
    weights_ref[...] = rows_ref[...].astype(bf16)


def join_kernel(place_ref, own_ref, got_ref, from_1, from_2, from_3, from_4, back_ref, out_ref, slabs):
    y, core = place_ref[0], place_ref[1]
    step = 1 + (Y - 2) * core

    def put(chip, same, other):
        first = 2 * lax.rem(chip, Y)
        slabs[first + core] = same
        slabs[first + 1 - core] = other

    put(y, own_ref[0, 7], got_ref[7])
    for k, from_ref in enumerate((from_1, from_2, from_3), 1):
        put(y + (Y - k) * step, from_ref[0], from_ref[2])
        put(y + k * step, back_ref[2 * k - 1], back_ref[2 * k - 2])
    put(y + Y // 2, from_4[0], from_4[1])
    out_ref[...] = jnp.concatenate([slabs[head][:, :HEAD_DIM] for head in range(HEADS)], axis=1)


def sum_kernel(parts_ref, grad_ref, squares_ref):
    total = parts_ref[0].astype(f32)
    for image in range(1, DP):
        total += parts_ref[image].astype(f32)
    for part in range(3):
        grad_ref[:, part * HEAD_DIM : (part + 1) * HEAD_DIM] = total[:, part * LANES : part * LANES + HEAD_DIM]
    squares_ref[...] = jnp.full(squares_ref.shape, jnp.sum(total * total))


def step_kernel(rate_ref, squares_ref, grad_ref, weight_ref, first_ref, second_ref, update_ref, new_first_ref, new_second_ref):
    squares = jnp.sum(squares_ref[...], axis=0)[:, :1]
    clip_factor = lax.rsqrt(squares / (D * HEADS * 3 * HEAD_DIM) + clip_epsilon)
    rate = rate_ref[0]
    for row in range(FEATS):
        clipped = grad_ref[row : row + 1, :] * clip_factor
        new_first = first_decay * first_ref[row] + (1.0 - first_decay) * clipped
        new_second = second_decay * second_ref[row] + (1.0 - second_decay) * clipped * clipped
        first_hat = new_first / (1.0 - first_decay**STEP)
        second_hat = new_second / (1.0 - second_decay**STEP)
        new_first_ref[row] = new_first
        new_second_ref[row] = new_second
        update_ref[row] = rate * (
            first_hat / (jnp.sqrt(second_hat) + adam_epsilon) + weight_decay * weight_ref[row]
        )


def dot_nt(left, right):
    return lax.dot_general(left, right, (((1,), (1,)), ((), ())), preferred_element_type=f32)


def dot(left, right):
    return lax.dot_general(left, right, (((1,), (0,)), ((), ())), preferred_element_type=f32)


def head_kernel(
    chosen_ref, place_ref, tokens_hbm, weights,
    grads, attended_ref, grad_ref,
    tokens, keys, values, queries, keys_t, values_t,
    key_grads, value_grads, joined_t, sems,
):
    copies = [
        pltpu.make_async_copy(
            tokens_hbm.at[pl.ds(b * BLOCK, BLOCK)], tokens.at[pl.ds(b * BLOCK, BLOCK)], sems.at[b]
        )
        for b in range(BLOCKS)
    ]
    copies[0].start()
    copies[1].start()
    y, core = place_ref[0], place_ref[1]
    key_grads[...] = jnp.zeros_like(key_grads)
    value_grads[...] = jnp.zeros_like(value_grads)
    for b in range(BLOCKS):
        rows = pl.ds(b * BLOCK, BLOCK)
        if b + 2 < BLOCKS:
            copies[b + 2].start()
        copies[b].wait()
        projected = dot(tokens[rows, :], weights[...]).astype(bf16)
        key = projected[:, LANES : 2 * LANES]
        value = projected[:, 2 * LANES :]
        keys[rows, :] = key
        values[rows, :] = value
        queries[rows, :] = projected[:, :LANES]
        keys_t[:, rows] = key.T
        values_t[:, rows] = value.T

    def front(b):
        here = pl.ds(b * BLOCK, BLOCK)
        query = queries[here, :]
        grad = grads[here, :]
        places = [pl.ds(pl.multiple_of(chosen_ref[3 * b + j] * BLOCK, BLOCK), BLOCK) for j in range(3)]
        scores = [dot_nt(keys[place, :], query) for place in places]
        prob_grads = [dot_nt(values[place, :], grad) for place in places]
        return b, here, query, grad, places, scores, prob_grads

    def middle(state):
        b, here, query, grad, places, scores, prob_grads = state
        top = jnp.max(jnp.maximum(jnp.maximum(scores[0], scores[1]), scores[2]), axis=0, keepdims=True)
        shifted = [jnp.exp2((score - top) * (score_scale * LOG2E)) for score in scores]
        total = jnp.sum(shifted[0] + shifted[1] + shifted[2], axis=0, keepdims=True)
        scale = 1.0 / total
        soft_low = [(part * scale).astype(bf16) for part in shifted]
        row_dot = scale * jnp.sum(
            shifted[0] * prob_grads[0] + shifted[1] * prob_grads[1] + shifted[2] * prob_grads[2],
            axis=0, keepdims=True,
        )
        grad_scale = scale * score_scale
        score_grads = [
            (part * (prob - row_dot) * grad_scale).astype(bf16) for part, prob in zip(shifted, prob_grads)
        ]
        return soft_low, score_grads

    def back(state, soft_low, score_grads):
        b, here, query, grad, places, _, _ = state
        attended_t = sum(dot(values_t[:, place], low) for place, low in zip(places, soft_low))
        query_grads_t = sum(dot(keys_t[:, place], part) for place, part in zip(places, score_grads))
        value_terms = [dot(low, grad) for low in soft_low]
        key_terms = [dot(part, query) for part in score_grads]
        for place, value_term, key_term in zip(places, value_terms, key_terms):
            value_grads[place, :] += value_term
            key_grads[place, :] += key_term
        joined_t[:LANES, here] = query_grads_t.astype(bf16)
        attended = attended_t.astype(bf16).T
        ahead = lax.rem((b + Y - y) * (1 + (Y - 2) * core), Y)
        for half in range(CORES):
            other = lax.rem(half + core, CORES)
            side = jnp.where(lax.rem(ahead, 4) == 0, other, jnp.where(ahead < 4, 0, 1))
            near = jnp.where(ahead < 4, 2 * ahead - 2 + other, 2 * (7 - ahead) + 1 - other)
            slot = jnp.where(ahead == 0, 7, jnp.where(ahead == 4, 6, near))
            attended_ref[side, slot] = attended[half * ROWS : (half + 1) * ROWS]

    states = [front(0)]
    for b in range(BLOCKS):
        if b + 1 < BLOCKS:
            states.append(front(b + 1))
        back(states[b], *middle(states[b]))
    for b in range(BLOCKS):
        rows = pl.ds(b * BLOCK, BLOCK)
        joined_t[LANES : 2 * LANES, rows] = key_grads[rows, :].astype(bf16).T
        joined_t[2 * LANES :, rows] = value_grads[rows, :].astype(bf16).T
    for start in range(0, D, 2 * LANES):
        part = dot(joined_t[...], tokens[:, start : start + 2 * LANES])
        grad_ref[start : start + 2 * LANES, :] = part.astype(bf16).T


def head_call(chosen, place, tokens, weights, grads):
    return pl.pallas_call(
        head_kernel,
        out_shape=(
            jax.ShapeDtypeStruct((CORES, Y, ROWS, LANES), bf16),
            jax.ShapeDtypeStruct((D, SLOTS), bf16),
        ),
        in_specs=[SMEM, SMEM, HBM, VMEM, VMEM],
        out_specs=(VMEM, VMEM),
        scratch_shapes=[
            pltpu.VMEM((PATCHES, D), bf16),
            pltpu.VMEM((PATCHES, LANES), bf16),
            pltpu.VMEM((PATCHES, LANES), bf16),
            pltpu.VMEM((PATCHES, LANES), bf16),
            pltpu.VMEM((LANES, PATCHES), bf16),
            pltpu.VMEM((LANES, PATCHES), bf16),
            pltpu.VMEM((PATCHES, LANES), f32),
            pltpu.VMEM((PATCHES, LANES), f32),
            pltpu.VMEM((SLOTS, PATCHES), bf16),
            pltpu.SemaphoreType.DMA((BLOCKS,)),
        ],
        compiler_params=params(46),
        name="head",
    )(chosen, place, tokens, weights, grads)


def join_call(place, blocks):
    return pl.pallas_call(
        join_kernel,
        out_shape=jax.ShapeDtypeStruct((ROWS, D), bf16),
        in_specs=[SMEM] + [VMEM] * len(blocks),
        out_specs=VMEM,
        scratch_shapes=[pltpu.VMEM((HEADS, ROWS, LANES), bf16)],
        compiler_params=params(16),
        name="join",
    )(place, *blocks)


def ring(size, step):
    return [(at, (at + step) % size) for at in range(size)]


def gather_weights(place, weight_low):
    by_z = [weight_low] + [lax.ppermute(weight_low, "z", ring(Z, -k)) for k in range(1, Z)]
    own = jnp.stack(by_z)
    left_1, left_2, right_1, right_2 = (lax.ppermute(own, "x", ring(X, k)) for k in (1, 2, -1, -2))
    left_3 = lax.ppermute(left_2, "x", ring(X, 1))
    right_3 = lax.ppermute(right_2, "x", ring(X, -1))
    far_first = lax.ppermute(left_2[: Z // 2], "x", ring(X, 2))
    far_second = lax.ppermute(right_2[Z // 2 :], "x", ring(X, -2))
    blocks = [own, left_1, left_2, left_3, right_1, right_2, right_3, far_first, far_second]
    return pl.pallas_call(
        place_kernel,
        out_shape=jax.ShapeDtypeStruct((D, SLOTS), bf16),
        in_specs=[SMEM] + [VMEM] * len(blocks),
        out_specs=VMEM,
        scratch_shapes=[pltpu.VMEM((D, SLOTS), f32)],
        compiler_params=params(24),
        name="place",
    )(place, *blocks)


def along_y(k):
    return [
        (y * CORES + core, (y + (1 - 2 * core) * k) % Y * CORES + core) for y in range(Y) for core in range(CORES)
    ]


def return_heads(slabs):
    got = lax.ppermute(slabs[1], "c", ring(CORES, 1))
    moved = [
        lax.ppermute(
            jnp.concatenate([slabs[0, 2 * k - 2 : 2 * k], got[2 * k - 2 : 2 * k]]), ("y", "c"), along_y(k)
        )
        for k in range(1, 4)
    ]
    far = lax.ppermute(jnp.stack([slabs[0, 6], got[6]]), ("y", "c"), along_y(4))
    back = lax.ppermute(jnp.concatenate([part[1::2] for part in moved]), "c", ring(CORES, 1))
    return [slabs, got, *moved, far, back]


def small_call(kernel, out_shape, *arrays, scalars=()):
    return pl.pallas_call(
        kernel,
        out_shape=out_shape,
        in_specs=[SMEM] * len(scalars) + [VMEM] * len(arrays),
        out_specs=jax.tree.map(lambda _: VMEM, out_shape),
        compiler_params=params(16),
    )(*scalars, *arrays)


def local(patches, cotangent, pattern, weight, first_moment, second_moment, layer_index):
    place = jnp.stack([lax.axis_index("y"), lax.axis_index("c"), lax.axis_index("z"), lax.axis_index("x")]).astype(jnp.int32)
    normed = small_call(norm_kernel, jax.ShapeDtypeStruct((ROWS, D), bf16), patches[0])
    gathered = lax.all_gather(normed, ("y", "c"), axis=0, tiled=True)

    slabs = small_call(split_kernel, jax.ShapeDtypeStruct((HEADS, ROWS, LANES), bf16), cotangent[0])
    grads = lax.all_to_all(slabs, ("y", "c"), 0, 0, tiled=True).reshape(PATCHES, LANES)
    weight_low = jnp.pad(
        weight.astype(bf16).reshape(FEATS, 3, HEAD_DIM), ((0, 0), (0, 0), (0, LANES - HEAD_DIM))
    ).reshape(FEATS, SLOTS)
    weight_low, _ = lax.optimization_barrier((weight_low, slabs))
    weights = gather_weights(place, weight_low)

    attended, grad_parts = head_call(pattern[:, 1], place, gathered, weights, grads)

    received = lax.all_to_all(grad_parts.reshape(DP, FEATS, SLOTS), ("z", "x"), 0, 0, tiled=True)
    received, *returned = lax.optimization_barrier((received, *return_heads(attended)))
    grad, squares = small_call(
        sum_kernel,
        (jax.ShapeDtypeStruct((FEATS, 3 * HEAD_DIM), f32), jax.ShapeDtypeStruct((DP, 1, LANES), f32)),
        received,
    )
    squares = jnp.sum(lax.all_to_all(squares, ("z", "x"), 0, 0, tiled=True), axis=0)
    squares = lax.all_to_all(jnp.broadcast_to(squares, (SEQ, 1, LANES)), ("y", "c"), 0, 0, tiled=True)
    attn_out = join_call(place, returned)

    rate = jnp.power(f32(layer_decay), (DEPTH - 1 - layer_index).astype(f32))
    update, new_first, new_second = small_call(
        step_kernel,
        (jax.ShapeDtypeStruct(weight.shape, f32),) * 3,
        squares, grad, weight, first_moment, second_moment,
        scalars=(rate.reshape(1),),
    )
    return (attn_out[None], update, new_first, new_second)


def solution(mesh):
    named = Mesh(mesh.devices.reshape(Z, X, Y, CORES), ("z", "x", "y", "c"))
    split = P(("z", "x"), ("y", "c"), None)
    return jax.shard_map(
        local,
        mesh=named,
        in_specs=(split, split, P(), split, split, split, P()),
        out_specs=(split, split, split, split),
        check_vma=False,
    )
```

```python
import jax
import jax.numpy as jnp
from jax import lax
from jax.experimental import pallas as pl
from jax.experimental.pallas import tpu as pltpu
from jax.sharding import Mesh
from jax.sharding import PartitionSpec as P

D = 1792
HEADS = 16
HEAD_DIM = 112
DEPTH = 56
STEP = 1000
PATCHES = 2048
BLOCK = 256
BLOCKS = PATCHES // BLOCK
LANES = 128
SLOTS = 3 * LANES
DP = 32
SEQ = 16
ROWS = PATCHES // SEQ
FEATS = D // DP
REST = (3 * HEAD_DIM - 2 * LANES) // 2
PACKED = 2 * FEATS + REST
Z, X, Y, CORES = 4, 8, 8, 2

norm_epsilon = 1e-06
clip_epsilon = 1e-06
first_decay = 0.9
second_decay = 0.999
adam_epsilon = 1e-08
weight_decay = 0.05
layer_decay = 0.9
LOG2E = 1.4426950408889634
score_scale = HEAD_DIM ** (-0.5)

f32 = jnp.float32
bf16 = jnp.bfloat16
VMEM = pl.BlockSpec(memory_space=pltpu.VMEM)
SMEM = pl.BlockSpec(memory_space=pltpu.SMEM)
HBM = pl.BlockSpec(memory_space=pltpu.HBM)


def params(megabytes):
    return pltpu.CompilerParams(vmem_limit_bytes=megabytes * 2**20)


def norm_kernel(patch_ref, normed_ref):
    for start in range(0, ROWS, 32):
        rows = pl.ds(start, 32)
        floats = patch_ref[rows, :].astype(f32)
        centred = floats - jnp.mean(floats, axis=-1, keepdims=True)
        spread = jnp.mean(centred * centred, axis=-1, keepdims=True)
        normed_ref[rows, :] = (centred * lax.rsqrt(spread + norm_epsilon)).astype(bf16)


def split_kernel(grad_ref, slabs_ref):
    empty = jnp.zeros((ROWS, LANES - HEAD_DIM), bf16)
    for head in range(HEADS):
        part = grad_ref[:, head * HEAD_DIM : (head + 1) * HEAD_DIM]
        slabs_ref[head] = jnp.concatenate([part, empty], axis=1)


def place_kernel(place_ref, *refs):
    block_refs, weights_ref, rows_ref = refs[:-2], refs[-2], refs[-1]
    z, x = place_ref[2], place_ref[3]
    for block_ref, shift, first in zip(block_refs, (0, -1, -2, -3, 1, 2, 3, 4, 4), (0,) * 8 + (2,)):
        for k in range(block_ref.shape[0]):
            owner = lax.rem(z + first + k, Z) * X + lax.rem(x + shift + X, X)
            rows_ref[pl.ds(pl.multiple_of(owner * FEATS, 8), FEATS), :] = block_ref[k].astype(f32)
    weights_ref[...] = rows_ref[...].astype(bf16)


def join_kernel(place_ref, own_ref, got_ref, from_1, from_2, from_3, from_4, back_ref, out_ref, slabs):
    y, core = place_ref[0], place_ref[1]
    step = 1 + (Y - 2) * core

    def put(chip, same, other):
        first = 2 * lax.rem(chip, Y)
        slabs[first + core] = same
        slabs[first + 1 - core] = other

    put(y, own_ref[0, 7], got_ref[7])
    for k, from_ref in enumerate((from_1, from_2, from_3), 1):
        put(y + (Y - k) * step, from_ref[0], from_ref[2])
        put(y + k * step, back_ref[2 * k - 1], back_ref[2 * k - 2])
    put(y + Y // 2, from_4[0], back_ref[6])
    out_ref[...] = jnp.concatenate([slabs[head][:, :HEAD_DIM] for head in range(HEADS)], axis=1)


def sum_kernel(parts_ref, grad_ref, squares_ref, turned):
    total = parts_ref[0].astype(f32)
    for image in range(1, DP):
        total += parts_ref[image].astype(f32)
    grad_ref[:, :LANES] = total[:FEATS]
    grad_ref[:, LANES : 2 * LANES] = total[FEATS : 2 * FEATS]
    turned[:REST, :FEATS] = total[2 * FEATS :, :FEATS]
    turned[REST : 2 * REST, :FEATS] = total[2 * FEATS :, FEATS : 2 * FEATS]
    grad_ref[:, 2 * LANES :] = turned[...].T[:FEATS, : 2 * REST]
    squares_ref[...] = jnp.full(squares_ref.shape, jnp.sum(total * total))


def step_kernel(rate_ref, squares_ref, grad_ref, weight_ref, first_ref, second_ref, update_ref, new_first_ref, new_second_ref):
    squares = jnp.sum(squares_ref[...], axis=0)[:, :1]
    clip_factor = lax.rsqrt(squares / (D * HEADS * 3 * HEAD_DIM) + clip_epsilon)
    rate = rate_ref[0]
    for row in range(FEATS):
        clipped = grad_ref[row : row + 1, :] * clip_factor
        new_first = first_decay * first_ref[row] + (1.0 - first_decay) * clipped
        new_second = second_decay * second_ref[row] + (1.0 - second_decay) * clipped * clipped
        first_hat = new_first / (1.0 - first_decay**STEP)
        second_hat = new_second / (1.0 - second_decay**STEP)
        new_first_ref[row] = new_first
        new_second_ref[row] = new_second
        update_ref[row] = rate * (
            first_hat / (jnp.sqrt(second_hat) + adam_epsilon) + weight_decay * weight_ref[row]
        )


def dot_nt(left, right):
    return lax.dot_general(left, right, (((1,), (1,)), ((), ())), preferred_element_type=f32)


def dot(left, right):
    return lax.dot_general(left, right, (((1,), (0,)), ((), ())), preferred_element_type=f32)


def head_kernel(
    chosen_ref, place_ref, tokens_hbm, weights,
    grads, attended_ref, grad_ref,
    tokens, keys, values, queries, keys_t, values_t,
    key_grads, value_grads, joined_t, grad_rows, grad_rest, sems,
):
    copies = [
        pltpu.make_async_copy(
            tokens_hbm.at[pl.ds(b * BLOCK, BLOCK)], tokens.at[pl.ds(b * BLOCK, BLOCK)], sems.at[b]
        )
        for b in range(BLOCKS)
    ]
    copies[0].start()
    copies[1].start()
    y, core = place_ref[0], place_ref[1]
    key_grads[...] = jnp.zeros_like(key_grads)
    value_grads[...] = jnp.zeros_like(value_grads)
    for b in range(BLOCKS):
        rows = pl.ds(b * BLOCK, BLOCK)
        if b + 2 < BLOCKS:
            copies[b + 2].start()
        copies[b].wait()
        projected = dot(tokens[rows, :], weights[...]).astype(bf16)
        key = projected[:, LANES : 2 * LANES]
        value = projected[:, 2 * LANES :]
        keys[rows, :] = key
        values[rows, :] = value
        queries[rows, :] = projected[:, :LANES]
        keys_t[:, rows] = key.T
        values_t[:, rows] = value.T

    def front(b):
        here = pl.ds(b * BLOCK, BLOCK)
        query = queries[here, :]
        grad = grads[here, :]
        places = [pl.ds(pl.multiple_of(chosen_ref[3 * b + j] * BLOCK, BLOCK), BLOCK) for j in range(3)]
        scores = [dot_nt(keys[place, :], query) for place in places]
        prob_grads = [dot_nt(values[place, :], grad) for place in places]
        return b, here, query, grad, places, scores, prob_grads

    def middle(state):
        b, here, query, grad, places, scores, prob_grads = state
        top = jnp.max(jnp.maximum(jnp.maximum(scores[0], scores[1]), scores[2]), axis=0, keepdims=True)
        shifted = [jnp.exp2((score - top) * (score_scale * LOG2E)) for score in scores]
        total = jnp.sum(shifted[0] + shifted[1] + shifted[2], axis=0, keepdims=True)
        scale = 1.0 / total
        soft_low = [(part * scale).astype(bf16) for part in shifted]
        row_dot = scale * jnp.sum(
            shifted[0] * prob_grads[0] + shifted[1] * prob_grads[1] + shifted[2] * prob_grads[2],
            axis=0, keepdims=True,
        )
        grad_scale = scale * score_scale
        score_grads = [
            (part * (prob - row_dot) * grad_scale).astype(bf16) for part, prob in zip(shifted, prob_grads)
        ]
        return soft_low, score_grads

    def back(state, soft_low, score_grads):
        b, here, query, grad, places, _, _ = state
        attended_t = sum(dot(values_t[:, place], low) for place, low in zip(places, soft_low))
        query_grads_t = sum(dot(keys_t[:, place], part) for place, part in zip(places, score_grads))
        value_terms = [dot(low, grad) for low in soft_low]
        key_terms = [dot(part, query) for part in score_grads]
        for place, value_term, key_term in zip(places, value_terms, key_terms):
            value_grads[place, :] += value_term
            key_grads[place, :] += key_term
        joined_t[:HEAD_DIM, here] = query_grads_t[:HEAD_DIM].astype(bf16)
        attended = attended_t.astype(bf16).T
        ahead = lax.rem((b + Y - y) * (1 + (Y - 2) * core), Y)
        for half in range(CORES):
            other = lax.rem(half + core, CORES)
            side = jnp.where(lax.rem(ahead, 4) == 0, other, jnp.where(ahead < 4, 0, 1))
            near = jnp.where(ahead < 4, 2 * ahead - 2 + other, 2 * (7 - ahead) + 1 - other)
            slot = jnp.where(ahead == 0, 7, jnp.where(ahead == 4, 6, near))
            attended_ref[side, slot] = attended[half * ROWS : (half + 1) * ROWS]

    states = [front(0)]
    for b in range(BLOCKS):
        if b + 1 < BLOCKS:
            states.append(front(b + 1))
        back(states[b], *middle(states[b]))
    for b in range(BLOCKS):
        rows = pl.ds(b * BLOCK, BLOCK)
        joined_t[HEAD_DIM : 2 * HEAD_DIM, rows] = key_grads[rows, :].T[:HEAD_DIM].astype(bf16)
        joined_t[2 * HEAD_DIM :, rows] = value_grads[rows, :].T[:HEAD_DIM].astype(bf16)
    for start in range(0, D, 2 * LANES):
        part = dot(joined_t[...], tokens[:, start : start + 2 * LANES])
        grad_rows[start : start + 2 * LANES, :] = part[: 2 * LANES].T
        grad_rest[:, start : start + 2 * LANES] = part[2 * LANES :]
    empty = jnp.zeros((REST, LANES - 2 * FEATS), f32)
    for chunk in range(DP):
        rows = pl.ds(chunk * FEATS, FEATS)
        rest = grad_rest[:, chunk * FEATS : (chunk + 1) * FEATS]
        packed = jnp.concatenate(
            [
                grad_rows[rows, :LANES],
                grad_rows[rows, LANES:],
                jnp.concatenate([rest[:REST], rest[REST:], empty], axis=1),
            ],
            axis=0,
        )
        grad_ref[chunk] = packed.astype(bf16)


def head_call(chosen, place, tokens, weights, grads):
    return pl.pallas_call(
        head_kernel,
        out_shape=(
            jax.ShapeDtypeStruct((CORES, Y, ROWS, LANES), bf16),
            jax.ShapeDtypeStruct((DP, PACKED, LANES), bf16),
        ),
        in_specs=[SMEM, SMEM, HBM, VMEM, VMEM],
        out_specs=(VMEM, VMEM),
        scratch_shapes=[
            pltpu.VMEM((PATCHES, D), bf16),
            pltpu.VMEM((PATCHES, LANES), bf16),
            pltpu.VMEM((PATCHES, LANES), bf16),
            pltpu.VMEM((PATCHES, LANES), bf16),
            pltpu.VMEM((LANES, PATCHES), bf16),
            pltpu.VMEM((LANES, PATCHES), bf16),
            pltpu.VMEM((PATCHES, LANES), f32),
            pltpu.VMEM((PATCHES, LANES), f32),
            pltpu.VMEM((3 * HEAD_DIM, PATCHES), bf16),
            pltpu.VMEM((D, 2 * LANES), f32),
            pltpu.VMEM((2 * REST, D), f32),
            pltpu.SemaphoreType.DMA((BLOCKS,)),
        ],
        compiler_params=params(46),
        name="head",
    )(chosen, place, tokens, weights, grads)


def join_call(place, blocks):
    return pl.pallas_call(
        join_kernel,
        out_shape=jax.ShapeDtypeStruct((ROWS, D), bf16),
        in_specs=[SMEM] + [VMEM] * len(blocks),
        out_specs=VMEM,
        scratch_shapes=[pltpu.VMEM((HEADS, ROWS, LANES), bf16)],
        compiler_params=params(16),
        name="join",
    )(place, *blocks)


def ring(size, step):
    return [(at, (at + step) % size) for at in range(size)]


def gather_weights(place, weight_low):
    by_z = [weight_low] + [lax.ppermute(weight_low, "z", ring(Z, -k)) for k in range(1, Z)]
    own = jnp.stack(by_z)
    left_1, left_2, right_1, right_2 = (lax.ppermute(own, "x", ring(X, k)) for k in (1, 2, -1, -2))
    left_3 = lax.ppermute(left_2, "x", ring(X, 1))
    right_3 = lax.ppermute(right_2, "x", ring(X, -1))
    far_first = lax.ppermute(left_2[: Z // 2], "x", ring(X, 2))
    far_second = lax.ppermute(right_2[Z // 2 :], "x", ring(X, -2))
    blocks = [own, left_1, left_2, left_3, right_1, right_2, right_3, far_first, far_second]
    return pl.pallas_call(
        place_kernel,
        out_shape=jax.ShapeDtypeStruct((D, SLOTS), bf16),
        in_specs=[SMEM] + [VMEM] * len(blocks),
        out_specs=VMEM,
        scratch_shapes=[pltpu.VMEM((D, SLOTS), f32)],
        compiler_params=params(24),
        name="place",
    )(place, *blocks)


def along_y(k):
    return [
        (y * CORES + core, (y + (1 - 2 * core) * k) % Y * CORES + core) for y in range(Y) for core in range(CORES)
    ]


def return_heads(slabs):
    far = lax.ppermute(slabs[:, 6], ("y", "c"), along_y(4))
    got = lax.ppermute(slabs[1], "c", ring(CORES, 1))
    moved = [
        lax.ppermute(
            jnp.concatenate([slabs[0, 2 * k - 2 : 2 * k], got[2 * k - 2 : 2 * k]]), ("y", "c"), along_y(k)
        )
        for k in range(1, 4)
    ]
    back = lax.ppermute(jnp.concatenate([*(part[1::2] for part in moved), far[1:]]), "c", ring(CORES, 1))
    return [slabs, got, *moved, far, back]


def small_call(kernel, out_shape, *arrays, scalars=()):
    return pl.pallas_call(
        kernel,
        out_shape=out_shape,
        in_specs=[SMEM] * len(scalars) + [VMEM] * len(arrays),
        out_specs=jax.tree.map(lambda _: VMEM, out_shape),
        compiler_params=params(16),
    )(*scalars, *arrays)


def local(patches, cotangent, pattern, weight, first_moment, second_moment, layer_index):
    place = jnp.stack([lax.axis_index("y"), lax.axis_index("c"), lax.axis_index("z"), lax.axis_index("x")]).astype(jnp.int32)
    normed = small_call(norm_kernel, jax.ShapeDtypeStruct((ROWS, D), bf16), patches[0])
    gathered = lax.all_gather(normed, ("y", "c"), axis=0, tiled=True)

    slabs = small_call(split_kernel, jax.ShapeDtypeStruct((HEADS, ROWS, LANES), bf16), cotangent[0])
    grads = lax.all_to_all(slabs, ("y", "c"), 0, 0, tiled=True).reshape(PATCHES, LANES)
    weight_low = jnp.pad(
        weight.astype(bf16).reshape(FEATS, 3, HEAD_DIM), ((0, 0), (0, 0), (0, LANES - HEAD_DIM))
    ).reshape(FEATS, SLOTS)
    weight_low, _ = lax.optimization_barrier((weight_low, slabs))
    weights = gather_weights(place, weight_low)

    attended, grad_parts = head_call(pattern[:, 1], place, gathered, weights, grads)

    received = lax.all_to_all(grad_parts, ("z", "x"), 0, 0, tiled=True)
    received, *returned = lax.optimization_barrier((received, *return_heads(attended)))
    grad, squares = pl.pallas_call(
        sum_kernel,
        out_shape=(
            jax.ShapeDtypeStruct((FEATS, 3 * HEAD_DIM), f32),
            jax.ShapeDtypeStruct((DP, 1, LANES), f32),
        ),
        in_specs=[VMEM],
        out_specs=(VMEM, VMEM),
        scratch_shapes=[pltpu.VMEM((LANES, LANES), f32)],
        compiler_params=params(16),
        name="sum",
    )(received)
    squares = jnp.sum(lax.all_to_all(squares, ("z", "x"), 0, 0, tiled=True), axis=0)
    squares = lax.all_to_all(jnp.broadcast_to(squares, (SEQ, 1, LANES)), ("y", "c"), 0, 0, tiled=True)
    attn_out = join_call(place, returned)

    rate = jnp.power(f32(layer_decay), (DEPTH - 1 - layer_index).astype(f32))
    update, new_first, new_second = small_call(
        step_kernel,
        (jax.ShapeDtypeStruct(weight.shape, f32),) * 3,
        squares, grad, weight, first_moment, second_moment,
        scalars=(rate.reshape(1),),
    )
    return (attn_out[None], update, new_first, new_second)


def solution(mesh):
    named = Mesh(mesh.devices.reshape(Z, X, Y, CORES), ("z", "x", "y", "c"))
    split = P(("z", "x"), ("y", "c"), None)
    return jax.shard_map(
        local,
        mesh=named,
        in_specs=(split, split, P(), split, split, split, P()),
        out_specs=(split, split, split, split),
        check_vma=False,
    )
```

```python
import jax
import jax.numpy as jnp
from jax import lax
from jax.experimental import pallas as pl
from jax.experimental.pallas import tpu as pltpu
from jax.sharding import Mesh
from jax.sharding import PartitionSpec as P

D = 1792
HEADS = 16
HEAD_DIM = 112
DEPTH = 56
STEP = 1000
PATCHES = 2048
BLOCK = 256
BLOCKS = PATCHES // BLOCK
LANES = 128
SLOTS = 3 * LANES
DP = 32
SEQ = 16
ROWS = PATCHES // SEQ
FEATS = D // DP
REST = (3 * HEAD_DIM - 2 * LANES) // 2
PACKED = 2 * FEATS + REST
Z, X, Y, CORES = 4, 8, 8, 2

norm_epsilon = 1e-06
clip_epsilon = 1e-06
first_decay = 0.9
second_decay = 0.999
adam_epsilon = 1e-08
weight_decay = 0.05
layer_decay = 0.9
LOG2E = 1.4426950408889634
score_scale = HEAD_DIM ** (-0.5)

f32 = jnp.float32
bf16 = jnp.bfloat16
VMEM = pl.BlockSpec(memory_space=pltpu.VMEM)
SMEM = pl.BlockSpec(memory_space=pltpu.SMEM)
HBM = pl.BlockSpec(memory_space=pltpu.HBM)


def params(megabytes):
    return pltpu.CompilerParams(vmem_limit_bytes=megabytes * 2**20)


def norm_kernel(patch_ref, normed_ref):
    for start in range(0, ROWS, 32):
        rows = pl.ds(start, 32)
        floats = patch_ref[rows, :].astype(f32)
        centred = floats - jnp.mean(floats, axis=-1, keepdims=True)
        spread = jnp.mean(centred * centred, axis=-1, keepdims=True)
        normed_ref[rows, :] = (centred * lax.rsqrt(spread + norm_epsilon)).astype(bf16)


def split_kernel(grad_ref, slabs_ref):
    empty = jnp.zeros((ROWS, LANES - HEAD_DIM), bf16)
    for head in range(HEADS):
        part = grad_ref[:, head * HEAD_DIM : (head + 1) * HEAD_DIM]
        slabs_ref[head] = jnp.concatenate([part, empty], axis=1).T[:HEAD_DIM]


def place_kernel(place_ref, *refs):
    block_refs, weights_ref, rows_ref = refs[:-2], refs[-2], refs[-1]
    z, x = place_ref[2], place_ref[3]
    for at, (block_ref, shift) in enumerate(zip(block_refs, (0, -1, -2, 1, 2, -3, 3))):
        for k in range(block_ref.shape[0]):
            ahead, along = (k, shift) if k < Z else (k - Z + (at - 5) * Z // 2, X // 2)
            owner = lax.rem(z + ahead, Z) * X + lax.rem(x + along + X, X)
            rows_ref[pl.ds(pl.multiple_of(owner * FEATS, 8), FEATS), :] = block_ref[k].astype(f32)
    weights_ref[...] = rows_ref[...].astype(bf16)


def join_kernel(place_ref, own_ref, got_ref, from_1, from_2, from_3, from_4, back_ref, out_ref, slabs):
    y, core = place_ref[0], place_ref[1]
    step = 1 + (Y - 2) * core

    def put(chip, same, other):
        first = 2 * lax.rem(chip, Y)
        slabs[first + core, :HEAD_DIM, :] = same
        slabs[first + 1 - core, :HEAD_DIM, :] = other

    put(y, own_ref[0, 7], got_ref[7])
    for k, from_ref in enumerate((from_1, from_2, from_3), 1):
        put(y + (Y - k) * step, from_ref[0], from_ref[2])
        put(y + k * step, back_ref[2 * k - 1], back_ref[2 * k - 2])
    put(y + Y // 2, from_4[0], back_ref[6])
    out_ref[...] = jnp.concatenate([slabs[head].T[:, :HEAD_DIM] for head in range(HEADS)], axis=1)


def sum_kernel(parts_ref, grad_ref, squares_ref, turned):
    total = parts_ref[0].astype(f32)
    for image in range(1, DP):
        total += parts_ref[image].astype(f32)
    grad_ref[:, :LANES] = total[:FEATS]
    grad_ref[:, LANES : 2 * LANES] = total[FEATS : 2 * FEATS]
    turned[:REST, :FEATS] = total[2 * FEATS :, :FEATS]
    turned[REST : 2 * REST, :FEATS] = total[2 * FEATS :, FEATS : 2 * FEATS]
    grad_ref[:, 2 * LANES :] = turned[...].T[:FEATS, : 2 * REST]
    squares_ref[...] = jnp.full(squares_ref.shape, jnp.sum(total * total))


def step_kernel(rate_ref, squares_ref, grad_ref, weight_ref, first_ref, second_ref, update_ref, new_first_ref, new_second_ref):
    squares = jnp.sum(squares_ref[...], axis=0)[:, :1]
    clip_factor = lax.rsqrt(squares / (D * HEADS * 3 * HEAD_DIM) + clip_epsilon)
    rate = rate_ref[0]
    for row in range(FEATS):
        clipped = grad_ref[row : row + 1, :] * clip_factor
        new_first = first_decay * first_ref[row] + (1.0 - first_decay) * clipped
        new_second = second_decay * second_ref[row] + (1.0 - second_decay) * clipped * clipped
        first_hat = new_first / (1.0 - first_decay**STEP)
        second_hat = new_second / (1.0 - second_decay**STEP)
        new_first_ref[row] = new_first
        new_second_ref[row] = new_second
        update_ref[row] = rate * (
            first_hat / (jnp.sqrt(second_hat) + adam_epsilon) + weight_decay * weight_ref[row]
        )


def dot_nt(left, right):
    return lax.dot_general(left, right, (((1,), (1,)), ((), ())), preferred_element_type=f32)


def dot(left, right):
    return lax.dot_general(left, right, (((1,), (0,)), ((), ())), preferred_element_type=f32)


def head_kernel(
    chosen_ref, place_ref, tokens_hbm, weights,
    grads_ref, attended_ref, grad_ref,
    tokens, grads_t, keys, values, queries, keys_t, values_t,
    key_grads, value_grads, joined_t, grad_rows, grad_rest, sems,
):
    copies = [
        pltpu.make_async_copy(
            tokens_hbm.at[pl.ds(b * BLOCK, BLOCK)], tokens.at[pl.ds(b * BLOCK, BLOCK)], sems.at[b]
        )
        for b in range(BLOCKS)
    ]
    copies[0].start()
    copies[1].start()
    y, core = place_ref[0], place_ref[1]
    grads_t[...] = jnp.zeros_like(grads_t)
    for part in range(SEQ):
        grads_t[:HEAD_DIM, part * ROWS : (part + 1) * ROWS] = grads_ref[part]
    key_grads[...] = jnp.zeros_like(key_grads)
    value_grads[...] = jnp.zeros_like(value_grads)
    for b in range(BLOCKS):
        rows = pl.ds(b * BLOCK, BLOCK)
        if b + 2 < BLOCKS:
            copies[b + 2].start()
        copies[b].wait()
        projected = dot(tokens[rows, :], weights[...]).astype(bf16)
        key = projected[:, LANES : 2 * LANES]
        value = projected[:, 2 * LANES :]
        keys[rows, :] = key
        values[rows, :] = value
        queries[rows, :] = projected[:, :LANES]
        keys_t[:, rows] = key.T
        values_t[:, rows] = value.T

    def front(b):
        here = pl.ds(b * BLOCK, BLOCK)
        query = queries[here, :]
        grad_t = grads_t[:, here]
        places = [pl.ds(pl.multiple_of(chosen_ref[3 * b + j] * BLOCK, BLOCK), BLOCK) for j in range(3)]
        scores = [dot_nt(keys[place, :], query) for place in places]
        prob_grads = [dot(values[place, :], grad_t) for place in places]
        return b, here, query, grad_t, places, scores, prob_grads

    def middle(state):
        b, here, query, grad_t, places, scores, prob_grads = state
        top = jnp.max(jnp.maximum(jnp.maximum(scores[0], scores[1]), scores[2]), axis=0, keepdims=True)
        shifted = [jnp.exp2((score - top) * (score_scale * LOG2E)) for score in scores]
        total = jnp.sum(shifted[0] + shifted[1] + shifted[2], axis=0, keepdims=True)
        scale = 1.0 / total
        soft_low = [(part * scale).astype(bf16) for part in shifted]
        row_dot = scale * jnp.sum(
            shifted[0] * prob_grads[0] + shifted[1] * prob_grads[1] + shifted[2] * prob_grads[2],
            axis=0, keepdims=True,
        )
        grad_scale = scale * score_scale
        score_grads = [
            (part * (prob - row_dot) * grad_scale).astype(bf16) for part, prob in zip(shifted, prob_grads)
        ]
        return soft_low, score_grads

    def back(state, soft_low, score_grads):
        b, here, query, grad_t, places, _, _ = state
        attended_t = sum(dot(values_t[:, place], low) for place, low in zip(places, soft_low))
        query_grads_t = sum(dot(keys_t[:, place], part) for place, part in zip(places, score_grads))
        value_terms = [dot_nt(low, grad_t) for low in soft_low]
        key_terms = [dot(part, query) for part in score_grads]
        for place, value_term, key_term in zip(places, value_terms, key_terms):
            value_grads[place, :] += value_term
            key_grads[place, :] += key_term
        joined_t[:HEAD_DIM, here] = query_grads_t[:HEAD_DIM].astype(bf16)
        attended = attended_t[:HEAD_DIM].astype(bf16)
        ahead = lax.rem((b + Y - y) * (1 + (Y - 2) * core), Y)
        for half in range(CORES):
            other = lax.rem(half + core, CORES)
            side = jnp.where(lax.rem(ahead, 4) == 0, other, jnp.where(ahead < 4, 0, 1))
            near = jnp.where(ahead < 4, 2 * ahead - 2 + other, 2 * (7 - ahead) + 1 - other)
            slot = jnp.where(ahead == 0, 7, jnp.where(ahead == 4, 6, near))
            attended_ref[side, slot] = attended[:, half * ROWS : (half + 1) * ROWS]

    states = [front(0)]
    for b in range(BLOCKS):
        if b + 1 < BLOCKS:
            states.append(front(b + 1))
        back(states[b], *middle(states[b]))
    for b in range(BLOCKS):
        rows = pl.ds(b * BLOCK, BLOCK)
        joined_t[HEAD_DIM : 2 * HEAD_DIM, rows] = key_grads[rows, :].T[:HEAD_DIM].astype(bf16)
        joined_t[2 * HEAD_DIM :, rows] = value_grads[rows, :].T[:HEAD_DIM].astype(bf16)
    for start in range(0, D, 2 * LANES):
        part = dot(joined_t[...], tokens[:, start : start + 2 * LANES])
        grad_rows[start : start + 2 * LANES, :] = part[: 2 * LANES].T
        grad_rest[:, start : start + 2 * LANES] = part[2 * LANES :]
    empty = jnp.zeros((REST, LANES - 2 * FEATS), f32)
    for chunk in range(DP):
        rows = pl.ds(chunk * FEATS, FEATS)
        rest = grad_rest[:, chunk * FEATS : (chunk + 1) * FEATS]
        packed = jnp.concatenate(
            [
                grad_rows[rows, :LANES],
                grad_rows[rows, LANES:],
                jnp.concatenate([rest[:REST], rest[REST:], empty], axis=1),
            ],
            axis=0,
        )
        grad_ref[chunk] = packed.astype(bf16)


def head_call(chosen, place, tokens, weights, grads):
    return pl.pallas_call(
        head_kernel,
        out_shape=(
            jax.ShapeDtypeStruct((CORES, Y, HEAD_DIM, ROWS), bf16),
            jax.ShapeDtypeStruct((DP, PACKED, LANES), bf16),
        ),
        in_specs=[SMEM, SMEM, HBM, VMEM, VMEM],
        out_specs=(VMEM, VMEM),
        scratch_shapes=[
            pltpu.VMEM((PATCHES, D), bf16),
            pltpu.VMEM((LANES, PATCHES), bf16),
            pltpu.VMEM((PATCHES, LANES), bf16),
            pltpu.VMEM((PATCHES, LANES), bf16),
            pltpu.VMEM((PATCHES, LANES), bf16),
            pltpu.VMEM((LANES, PATCHES), bf16),
            pltpu.VMEM((LANES, PATCHES), bf16),
            pltpu.VMEM((PATCHES, LANES), f32),
            pltpu.VMEM((PATCHES, LANES), f32),
            pltpu.VMEM((3 * HEAD_DIM, PATCHES), bf16),
            pltpu.VMEM((D, 2 * LANES), f32),
            pltpu.VMEM((2 * REST, D), f32),
            pltpu.SemaphoreType.DMA((BLOCKS,)),
        ],
        compiler_params=params(46),
        name="head",
    )(chosen, place, tokens, weights, grads)


def join_call(place, blocks):
    return pl.pallas_call(
        join_kernel,
        out_shape=jax.ShapeDtypeStruct((ROWS, D), bf16),
        in_specs=[SMEM] + [VMEM] * len(blocks),
        out_specs=VMEM,
        scratch_shapes=[pltpu.VMEM((HEADS, LANES, ROWS), bf16)],
        compiler_params=params(16),
        name="join",
    )(place, *blocks)


def ring(size, step):
    return [(at, (at + step) % size) for at in range(size)]


def gather_weights(place, weight_low, before):
    by_z = [weight_low] + [lax.ppermute(weight_low, "z", ring(Z, -k)) for k in range(1, Z)]
    own, before = lax.optimization_barrier((jnp.stack(by_z), before))
    left_1, left_2, right_1, right_2 = (lax.ppermute(own, "x", ring(X, k)) for k in (1, 2, -1, -2))
    left_beyond = lax.ppermute(jnp.concatenate([left_1, left_2[: Z // 2]]), "x", ring(X, 2))
    right_beyond = lax.ppermute(jnp.concatenate([right_1, right_2[Z // 2 :]]), "x", ring(X, -2))
    blocks = [own, left_1, left_2, right_1, right_2, left_beyond, right_beyond]
    weights = pl.pallas_call(
        place_kernel,
        out_shape=jax.ShapeDtypeStruct((D, SLOTS), bf16),
        in_specs=[SMEM] + [VMEM] * len(blocks),
        out_specs=VMEM,
        scratch_shapes=[pltpu.VMEM((D, SLOTS), f32)],
        compiler_params=params(24),
        name="place",
    )(place, *blocks)
    return weights, before


def along_y(k):
    return [
        (y * CORES + core, (y + (1 - 2 * core) * k) % Y * CORES + core) for y in range(Y) for core in range(CORES)
    ]


def return_heads(slabs):
    far = lax.ppermute(slabs[:, 6], ("y", "c"), along_y(4))
    got = lax.ppermute(slabs[1], "c", ring(CORES, 1))
    moved = [
        lax.ppermute(
            jnp.concatenate([slabs[0, 2 * k - 2 : 2 * k], got[2 * k - 2 : 2 * k]]), ("y", "c"), along_y(k)
        )
        for k in range(1, 4)
    ]
    back = lax.ppermute(jnp.concatenate([*(part[1::2] for part in moved), far[1:]]), "c", ring(CORES, 1))
    return [slabs, got, *moved, far, back]


def small_call(kernel, out_shape, *arrays, scalars=()):
    return pl.pallas_call(
        kernel,
        out_shape=out_shape,
        in_specs=[SMEM] * len(scalars) + [VMEM] * len(arrays),
        out_specs=jax.tree.map(lambda _: VMEM, out_shape),
        compiler_params=params(16),
    )(*scalars, *arrays)


def local(patches, cotangent, pattern, weight, first_moment, second_moment, layer_index):
    place = jnp.stack([lax.axis_index("y"), lax.axis_index("c"), lax.axis_index("z"), lax.axis_index("x")]).astype(jnp.int32)
    normed = small_call(norm_kernel, jax.ShapeDtypeStruct((ROWS, D), bf16), patches[0])
    gathered = lax.all_gather(normed, ("y", "c"), axis=0, tiled=True)

    slabs = small_call(split_kernel, jax.ShapeDtypeStruct((HEADS, HEAD_DIM, ROWS), bf16), cotangent[0])
    grads = lax.all_to_all(slabs, ("y", "c"), 0, 0, tiled=True)
    weight_low = jnp.pad(
        weight.astype(bf16).reshape(FEATS, 3, HEAD_DIM), ((0, 0), (0, 0), (0, LANES - HEAD_DIM))
    ).reshape(FEATS, SLOTS)
    weight_low, _ = lax.optimization_barrier((weight_low, slabs))
    weights, grads = gather_weights(place, weight_low, grads)

    attended, grad_parts = head_call(pattern[:, 1], place, gathered, weights, grads)

    received = lax.all_to_all(grad_parts, ("z", "x"), 0, 0, tiled=True)
    received, *returned = lax.optimization_barrier((received, *return_heads(attended)))
    grad, squares = pl.pallas_call(
        sum_kernel,
        out_shape=(
            jax.ShapeDtypeStruct((FEATS, 3 * HEAD_DIM), f32),
            jax.ShapeDtypeStruct((DP, 1, LANES), f32),
        ),
        in_specs=[VMEM],
        out_specs=(VMEM, VMEM),
        scratch_shapes=[pltpu.VMEM((LANES, LANES), f32)],
        compiler_params=params(16),
        name="sum",
    )(received)
    squares = jnp.sum(lax.all_to_all(squares, ("z", "x"), 0, 0, tiled=True), axis=0)
    squares = lax.all_to_all(jnp.broadcast_to(squares, (SEQ, 1, LANES)), ("y", "c"), 0, 0, tiled=True)
    attn_out = join_call(place, returned)

    rate = jnp.power(f32(layer_decay), (DEPTH - 1 - layer_index).astype(f32))
    update, new_first, new_second = small_call(
        step_kernel,
        (jax.ShapeDtypeStruct(weight.shape, f32),) * 3,
        squares, grad, weight, first_moment, second_moment,
        scalars=(rate.reshape(1),),
    )
    return (attn_out[None], update, new_first, new_second)


def solution(mesh):
    named = Mesh(mesh.devices.reshape(Z, X, Y, CORES), ("z", "x", "y", "c"))
    split = P(("z", "x"), ("y", "c"), None)
    return jax.shard_map(
        local,
        mesh=named,
        in_specs=(split, split, P(), split, split, split, P()),
        out_specs=(split, split, split, split),
        check_vma=False,
    )
```

```python
import jax
import jax.numpy as jnp
from jax import lax
from jax.experimental import pallas as pl
from jax.experimental.pallas import tpu as pltpu
from jax.sharding import Mesh
from jax.sharding import PartitionSpec as P

D = 1792
HEADS = 16
HEAD_DIM = 112
DEPTH = 56
STEP = 1000
PATCHES = 2048
BLOCK = 256
BLOCKS = PATCHES // BLOCK
LANES = 128
SLOTS = 3 * LANES
DP = 32
SEQ = 16
ROWS = PATCHES // SEQ
FEATS = D // DP
REST = (3 * HEAD_DIM - 2 * LANES) // 2
PACKED = 2 * FEATS + REST
Z, X, Y, CORES = 4, 8, 8, 2

norm_epsilon = 1e-06
clip_epsilon = 1e-06
first_decay = 0.9
second_decay = 0.999
adam_epsilon = 1e-08
weight_decay = 0.05
layer_decay = 0.9
LOG2E = 1.4426950408889634
score_scale = HEAD_DIM ** (-0.5)

f32 = jnp.float32
bf16 = jnp.bfloat16
VMEM = pl.BlockSpec(memory_space=pltpu.VMEM)
SMEM = pl.BlockSpec(memory_space=pltpu.SMEM)
HBM = pl.BlockSpec(memory_space=pltpu.HBM)


def params(megabytes):
    return pltpu.CompilerParams(vmem_limit_bytes=megabytes * 2**20)


def norm_kernel(patch_ref, normed_ref):
    for start in range(0, ROWS, 32):
        rows = pl.ds(start, 32)
        floats = patch_ref[rows, :].astype(f32)
        centred = floats - jnp.mean(floats, axis=-1, keepdims=True)
        spread = jnp.mean(centred * centred, axis=-1, keepdims=True)
        normed_ref[rows, :] = (centred * lax.rsqrt(spread + norm_epsilon)).astype(bf16)


def split_kernel(grad_ref, slabs_ref):
    empty = jnp.zeros((ROWS, LANES - HEAD_DIM), bf16)
    for head in range(HEADS):
        part = grad_ref[:, head * HEAD_DIM : (head + 1) * HEAD_DIM]
        slabs_ref[head] = jnp.concatenate([part, empty], axis=1).T[:HEAD_DIM]


def place_weights(place_ref, block_refs, weights_ref, rows_ref):
    z, x = place_ref[2], place_ref[3]
    for at, (block_ref, shift) in enumerate(zip(block_refs, (0, -1, -2, 1, 2, -3, 3))):
        for k in range(block_ref.shape[0]):
            ahead, along = (k, shift) if k < Z else (k - Z + (at - 5) * Z // 2, X // 2)
            owner = lax.rem(z + ahead, Z) * X + lax.rem(x + along + X, X)
            rows_ref[pl.ds(pl.multiple_of(owner * FEATS, 8), FEATS), :] = block_ref[k].astype(f32)
    weights_ref[...] = rows_ref[...].astype(bf16)


def join_kernel(place_ref, own_ref, got_ref, from_1, from_2, from_3, from_4, back_ref, out_ref, slabs):
    y, core = place_ref[0], place_ref[1]
    step = 1 + (Y - 2) * core

    def put(chip, same, other):
        first = 2 * lax.rem(chip, Y)
        slabs[first + core, :HEAD_DIM, :] = same
        slabs[first + 1 - core, :HEAD_DIM, :] = other

    put(y, own_ref[0, 7], got_ref[7])
    for k, from_ref in enumerate((from_1, from_2, from_3), 1):
        put(y + (Y - k) * step, from_ref[0], from_ref[2])
        put(y + k * step, back_ref[2 * k - 1], back_ref[2 * k - 2])
    put(y + Y // 2, from_4[0], back_ref[6])
    out_ref[...] = jnp.concatenate([slabs[head].T[:, :HEAD_DIM] for head in range(HEADS)], axis=1)


def sum_kernel(parts_ref, grad_ref, squares_ref, turned):
    total = parts_ref[0].astype(f32)
    for image in range(1, DP):
        total += parts_ref[image].astype(f32)
    grad_ref[:, :LANES] = total[:FEATS]
    grad_ref[:, LANES : 2 * LANES] = total[FEATS : 2 * FEATS]
    turned[:REST, :FEATS] = total[2 * FEATS :, :FEATS]
    turned[REST : 2 * REST, :FEATS] = total[2 * FEATS :, FEATS : 2 * FEATS]
    grad_ref[:, 2 * LANES :] = turned[...].T[:FEATS, : 2 * REST]
    squares_ref[...] = jnp.full(squares_ref.shape, jnp.sum(total * total))


def step_kernel(rate_ref, squares_ref, grad_ref, weight_ref, first_ref, second_ref, update_ref, new_first_ref, new_second_ref):
    squares = jnp.sum(squares_ref[...], axis=0)[:, :1]
    clip_factor = lax.rsqrt(squares / (D * HEADS * 3 * HEAD_DIM) + clip_epsilon)
    rate = rate_ref[0]
    for row in range(FEATS):
        clipped = grad_ref[row : row + 1, :] * clip_factor
        new_first = first_decay * first_ref[row] + (1.0 - first_decay) * clipped
        new_second = second_decay * second_ref[row] + (1.0 - second_decay) * clipped * clipped
        first_hat = new_first / (1.0 - first_decay**STEP)
        second_hat = new_second / (1.0 - second_decay**STEP)
        new_first_ref[row] = new_first
        new_second_ref[row] = new_second
        update_ref[row] = rate * (
            first_hat / (jnp.sqrt(second_hat) + adam_epsilon) + weight_decay * weight_ref[row]
        )


def dot_nt(left, right):
    return lax.dot_general(left, right, (((1,), (1,)), ((), ())), preferred_element_type=f32)


def dot(left, right):
    return lax.dot_general(left, right, (((1,), (0,)), ((), ())), preferred_element_type=f32)


def head_kernel(
    chosen_ref, place_ref, tokens_hbm, own, left_1, left_2, right_1, right_2, left_beyond, right_beyond,
    grads_ref, attended_ref, grad_ref,
    tokens, weights, weight_rows, grads_t, keys, values, queries, keys_t, values_t,
    key_grads, value_grads, joined_t, grad_rows, grad_rest, sems,
):
    copies = [
        pltpu.make_async_copy(
            tokens_hbm.at[pl.ds(b * BLOCK, BLOCK)], tokens.at[pl.ds(b * BLOCK, BLOCK)], sems.at[b]
        )
        for b in range(BLOCKS)
    ]
    copies[0].start()
    copies[1].start()
    place_weights(
        place_ref, (own, left_1, left_2, right_1, right_2, left_beyond, right_beyond), weights, weight_rows
    )
    y, core = place_ref[0], place_ref[1]
    grads_t[...] = jnp.zeros_like(grads_t)
    for part in range(SEQ):
        grads_t[:HEAD_DIM, part * ROWS : (part + 1) * ROWS] = grads_ref[part]
    key_grads[...] = jnp.zeros_like(key_grads)
    value_grads[...] = jnp.zeros_like(value_grads)
    for b in range(BLOCKS):
        rows = pl.ds(b * BLOCK, BLOCK)
        if b + 2 < BLOCKS:
            copies[b + 2].start()
        copies[b].wait()
        projected = dot(tokens[rows, :], weights[...]).astype(bf16)
        key = projected[:, LANES : 2 * LANES]
        value = projected[:, 2 * LANES :]
        keys[rows, :] = key
        values[rows, :] = value
        queries[rows, :] = projected[:, :LANES]
        keys_t[:, rows] = key.T
        values_t[:, rows] = value.T

    def front(b):
        here = pl.ds(b * BLOCK, BLOCK)
        query = queries[here, :]
        grad_t = grads_t[:, here]
        places = [pl.ds(pl.multiple_of(chosen_ref[3 * b + j] * BLOCK, BLOCK), BLOCK) for j in range(3)]
        scores = [dot_nt(keys[place, :], query) for place in places]
        prob_grads = [dot(values[place, :], grad_t) for place in places]
        return b, here, query, grad_t, places, scores, prob_grads

    def middle(state):
        b, here, query, grad_t, places, scores, prob_grads = state
        top = jnp.max(jnp.maximum(jnp.maximum(scores[0], scores[1]), scores[2]), axis=0, keepdims=True)
        shifted = [jnp.exp2((score - top) * (score_scale * LOG2E)) for score in scores]
        total = jnp.sum(shifted[0] + shifted[1] + shifted[2], axis=0, keepdims=True)
        scale = 1.0 / total
        soft_low = [(part * scale).astype(bf16) for part in shifted]
        row_dot = scale * jnp.sum(
            shifted[0] * prob_grads[0] + shifted[1] * prob_grads[1] + shifted[2] * prob_grads[2],
            axis=0, keepdims=True,
        )
        grad_scale = scale * score_scale
        score_grads = [
            (part * (prob - row_dot) * grad_scale).astype(bf16) for part, prob in zip(shifted, prob_grads)
        ]
        return soft_low, score_grads

    def back(state, soft_low, score_grads):
        b, here, query, grad_t, places, _, _ = state
        attended_t = sum(dot(values_t[:, place], low) for place, low in zip(places, soft_low))
        query_grads_t = sum(dot(keys_t[:, place], part) for place, part in zip(places, score_grads))
        value_terms = [dot_nt(low, grad_t) for low in soft_low]
        key_terms = [dot(part, query) for part in score_grads]
        for place, value_term, key_term in zip(places, value_terms, key_terms):
            value_grads[place, :] += value_term
            key_grads[place, :] += key_term
        joined_t[:HEAD_DIM, here] = query_grads_t[:HEAD_DIM].astype(bf16)
        attended = attended_t[:HEAD_DIM].astype(bf16)
        ahead = lax.rem((b + Y - y) * (1 + (Y - 2) * core), Y)
        for half in range(CORES):
            other = lax.rem(half + core, CORES)
            side = jnp.where(lax.rem(ahead, 4) == 0, other, jnp.where(ahead < 4, 0, 1))
            near = jnp.where(ahead < 4, 2 * ahead - 2 + other, 2 * (7 - ahead) + 1 - other)
            slot = jnp.where(ahead == 0, 7, jnp.where(ahead == 4, 6, near))
            attended_ref[side, slot] = attended[:, half * ROWS : (half + 1) * ROWS]

    states = [front(0)]
    for b in range(BLOCKS):
        if b + 1 < BLOCKS:
            states.append(front(b + 1))
        back(states[b], *middle(states[b]))
    for b in range(BLOCKS):
        rows = pl.ds(b * BLOCK, BLOCK)
        joined_t[HEAD_DIM : 2 * HEAD_DIM, rows] = key_grads[rows, :].T[:HEAD_DIM].astype(bf16)
        joined_t[2 * HEAD_DIM :, rows] = value_grads[rows, :].T[:HEAD_DIM].astype(bf16)
    for start in range(0, D, 2 * LANES):
        part = dot(joined_t[...], tokens[:, start : start + 2 * LANES])
        grad_rows[start : start + 2 * LANES, :] = part[: 2 * LANES].T
        grad_rest[:, start : start + 2 * LANES] = part[2 * LANES :]
    empty = jnp.zeros((REST, LANES - 2 * FEATS), f32)
    for chunk in range(DP):
        rows = pl.ds(chunk * FEATS, FEATS)
        rest = grad_rest[:, chunk * FEATS : (chunk + 1) * FEATS]
        packed = jnp.concatenate(
            [
                grad_rows[rows, :LANES],
                grad_rows[rows, LANES:],
                jnp.concatenate([rest[:REST], rest[REST:], empty], axis=1),
            ],
            axis=0,
        )
        grad_ref[chunk] = packed.astype(bf16)


def head_call(chosen, place, tokens, weights, grads):
    return pl.pallas_call(
        head_kernel,
        out_shape=(
            jax.ShapeDtypeStruct((CORES, Y, HEAD_DIM, ROWS), bf16),
            jax.ShapeDtypeStruct((DP, PACKED, LANES), bf16),
        ),
        in_specs=[SMEM, SMEM, HBM] + [VMEM] * 8,
        out_specs=(VMEM, VMEM),
        scratch_shapes=[
            pltpu.VMEM((PATCHES, D), bf16),
            pltpu.VMEM((D, SLOTS), bf16),
            pltpu.VMEM((D, SLOTS), f32),
            pltpu.VMEM((LANES, PATCHES), bf16),
            pltpu.VMEM((PATCHES, LANES), bf16),
            pltpu.VMEM((PATCHES, LANES), bf16),
            pltpu.VMEM((PATCHES, LANES), bf16),
            pltpu.VMEM((LANES, PATCHES), bf16),
            pltpu.VMEM((LANES, PATCHES), bf16),
            pltpu.VMEM((PATCHES, LANES), f32),
            pltpu.VMEM((PATCHES, LANES), f32),
            pltpu.VMEM((3 * HEAD_DIM, PATCHES), bf16),
            pltpu.VMEM((D, 2 * LANES), f32),
            pltpu.VMEM((2 * REST, D), f32),
            pltpu.SemaphoreType.DMA((BLOCKS,)),
        ],
        compiler_params=params(46),
        name="head",
    )(chosen, place, tokens, *weights, grads)


def join_call(place, blocks):
    return pl.pallas_call(
        join_kernel,
        out_shape=jax.ShapeDtypeStruct((ROWS, D), bf16),
        in_specs=[SMEM] + [VMEM] * len(blocks),
        out_specs=VMEM,
        scratch_shapes=[pltpu.VMEM((HEADS, LANES, ROWS), bf16)],
        compiler_params=params(16),
        name="join",
    )(place, *blocks)


def ring(size, step):
    return [(at, (at + step) % size) for at in range(size)]


def gather_weights(weight_low, before):
    by_z = [weight_low] + [lax.ppermute(weight_low, "z", ring(Z, -k)) for k in range(1, Z)]
    own, before = lax.optimization_barrier((jnp.stack(by_z), before))
    left_1, left_2, right_1, right_2 = (lax.ppermute(own, "x", ring(X, k)) for k in (1, 2, -1, -2))
    left_beyond = lax.ppermute(jnp.concatenate([left_1, left_2[: Z // 2]]), "x", ring(X, 2))
    right_beyond = lax.ppermute(jnp.concatenate([right_1, right_2[Z // 2 :]]), "x", ring(X, -2))
    blocks = [own, left_1, left_2, right_1, right_2, left_beyond, right_beyond]
    return blocks, before


def along_y(k):
    return [
        (y * CORES + core, (y + (1 - 2 * core) * k) % Y * CORES + core) for y in range(Y) for core in range(CORES)
    ]


def return_heads(slabs):
    far = lax.ppermute(slabs[:, 6], ("y", "c"), along_y(4))
    got = lax.ppermute(slabs[1], "c", ring(CORES, 1))
    moved = [
        lax.ppermute(
            jnp.concatenate([slabs[0, 2 * k - 2 : 2 * k], got[2 * k - 2 : 2 * k]]), ("y", "c"), along_y(k)
        )
        for k in range(1, 4)
    ]
    back = lax.ppermute(jnp.concatenate([*(part[1::2] for part in moved), far[1:]]), "c", ring(CORES, 1))
    return [slabs, got, *moved, far, back]


def small_call(kernel, out_shape, *arrays, scalars=()):
    return pl.pallas_call(
        kernel,
        out_shape=out_shape,
        in_specs=[SMEM] * len(scalars) + [VMEM] * len(arrays),
        out_specs=jax.tree.map(lambda _: VMEM, out_shape),
        compiler_params=params(16),
    )(*scalars, *arrays)


def local(patches, cotangent, pattern, weight, first_moment, second_moment, layer_index):
    place = jnp.stack([lax.axis_index("y"), lax.axis_index("c"), lax.axis_index("z"), lax.axis_index("x")]).astype(jnp.int32)
    normed = small_call(norm_kernel, jax.ShapeDtypeStruct((ROWS, D), bf16), patches[0])
    gathered = lax.all_gather(normed, ("y", "c"), axis=0, tiled=True)

    slabs = small_call(split_kernel, jax.ShapeDtypeStruct((HEADS, HEAD_DIM, ROWS), bf16), cotangent[0])
    grads = lax.all_to_all(slabs, ("y", "c"), 0, 0, tiled=True)
    weight_low = jnp.pad(
        weight.astype(bf16).reshape(FEATS, 3, HEAD_DIM), ((0, 0), (0, 0), (0, LANES - HEAD_DIM))
    ).reshape(FEATS, SLOTS)
    weight_low, _ = lax.optimization_barrier((weight_low, slabs))
    weights, grads = gather_weights(weight_low, grads)

    attended, grad_parts = head_call(pattern[:, 1], place, gathered, weights, grads)

    received = lax.all_to_all(grad_parts, ("z", "x"), 0, 0, tiled=True)
    received, *returned = lax.optimization_barrier((received, *return_heads(attended)))
    grad, squares = pl.pallas_call(
        sum_kernel,
        out_shape=(
            jax.ShapeDtypeStruct((FEATS, 3 * HEAD_DIM), f32),
            jax.ShapeDtypeStruct((DP, 1, LANES), f32),
        ),
        in_specs=[VMEM],
        out_specs=(VMEM, VMEM),
        scratch_shapes=[pltpu.VMEM((LANES, LANES), f32)],
        compiler_params=params(16),
        name="sum",
    )(received)
    squares = jnp.sum(lax.all_to_all(squares, ("z", "x"), 0, 0, tiled=True), axis=0)
    squares = lax.all_to_all(jnp.broadcast_to(squares, (SEQ, 1, LANES)), ("y", "c"), 0, 0, tiled=True)
    attn_out = join_call(place, returned)

    rate = jnp.power(f32(layer_decay), (DEPTH - 1 - layer_index).astype(f32))
    update, new_first, new_second = small_call(
        step_kernel,
        (jax.ShapeDtypeStruct(weight.shape, f32),) * 3,
        squares, grad, weight, first_moment, second_moment,
        scalars=(rate.reshape(1),),
    )
    return (attn_out[None], update, new_first, new_second)


def solution(mesh):
    named = Mesh(mesh.devices.reshape(Z, X, Y, CORES), ("z", "x", "y", "c"))
    split = P(("z", "x"), ("y", "c"), None)
    return jax.shard_map(
        local,
        mesh=named,
        in_specs=(split, split, P(), split, split, split, P()),
        out_specs=(split, split, split, split),
        check_vma=False,
    )
```
